512 devices in a mesh: row: 32 (over z, core), col: 16 (over x, y).
Axes of the slice: x: 4, y: 4, z: 16, core: 2. Of those that a mesh axis runs over, the one named last changes fastest.
Arguments:
- tiles: float32 [4096, 128, 128], P(('row', 'col')), may hold values from -0.48 to 0.48
- tile_rows: int32 [4096], P(('row', 'col')), may hold values from 0 to 255, as said below
- tile_cols: int32 [4096], P(('row', 'col')), may hold values from 0 to 511
- tile_count: int32 [512], P(('row', 'col')), may hold values from 1 to 8, as said below
- energy: float32 [1048576], P(('row', 'col')), may hold values from 0.4 to 10
- basis_block: float32 [4, 1048576], P(None, ('row', 'col')), may hold values from -14 to 14
- previous_block: float32 [4, 1048576], P(None, ('row', 'col')), may hold values from -6 to 6
- coupling: float32 [4, 4], replicated, may hold values from -2.5 to 2.5
Outputs:
- next_block: float32 [4, 1048576], P(None, ('row', 'col'))
- alpha: float32 [4, 4], replicated
- beta: float32 [4, 4], replicated
The draws below stay inside these ranges and needn't reach their ends.
Inputs may be any that keep to these rules, and one draw needn't show every extreme that they name: `tile_rows`: every placed tile lies on or above the tile diagonal of the 1048576 x 1048576 matrix; slots may place the same tile more than once, and their tiles add. `tile_count`: the first device holds 8 live slots.
All inputs are finite; a program needn't handle non-finite values.
Results may differ from the reference program's by a relative error of at most 0.0003.
Values sent between devices are 32-bit elements; how exact they have to be, the bound alone decides.
A program may use at most 128 MiB of HBM per device.

```python
import jax
import jax.numpy as jnp
from jax import lax

VEC_DEV = 2048
CAP = 8
K = 4
TILE = 128
N = 1048576
N_ROW = 32
N_COL = 16
DEVICES = 512


def pattern(key):
    key = jax.random.fold_in(key, 11)
    keys = jax.random.split(key, 4)
    total = N_ROW * N_COL * CAP
    per_seg = VEC_DEV // TILE
    device = jnp.arange(total, dtype=jnp.int32) // CAP
    row_index = device // N_COL
    col_index = device % N_COL
    segment = jax.random.randint(keys[0], (total,), 0, N_COL)
    row_off = jax.random.randint(keys[1], (total,), 0, per_seg)
    spread = jax.random.randint(keys[2], (total,), 0, 1 << 20)
    col_row = row_index + spread % (N_ROW - row_index)
    col_off = jax.random.randint(keys[3], (total,), 0, per_seg)
    same = col_row == row_index
    segment = jnp.where(same, jnp.minimum(segment, col_index), segment)
    row_off = jnp.where(same & (segment == col_index), jnp.minimum(row_off, col_off), row_off)
    return ((segment * per_seg + row_off).astype(jnp.int32), (col_row * per_seg + col_off).astype(jnp.int32))


def draw_tile_rows(key, part):
    return pattern(key)[0]


def draw_tile_cols(key, part):
    return pattern(key)[1]


def draw_tile_count(key, part):
    key = jax.random.fold_in(key, 23)
    device = jnp.arange(N_ROW * N_COL, dtype=jnp.int32)
    row_index = device // N_COL
    base = CAP - row_index * CAP // N_ROW
    jitter = jax.random.randint(key, (N_ROW * N_COL,), 0, CAP // 4 + 2)
    count = jnp.maximum(base - jitter, 1)
    return jnp.where(device == 0, CAP, count).astype(jnp.int32)


def draw_energy(key, part):
    key = jax.random.fold_in(key, 37)
    ramp = 1.0 + 3.0 * jnp.arange(N, dtype=jnp.float32) / N
    factor = jnp.exp(0.35 * jnp.clip(jax.random.normal(key, (N,), jnp.float32), -2.5, 2.5))
    return (ramp * factor).astype(jnp.float32)


def draw_basis_block(key, part):
    key = jax.random.fold_in(key, 41)
    keys = jax.random.split(key, 3)
    common = jnp.clip(jax.random.normal(keys[0], (N,), jnp.float32), -4.0, 4.0)
    own = jnp.clip(jax.random.normal(keys[1], (K, N), jnp.float32), -4.0, 4.0)
    scale = jnp.exp(jax.random.uniform(keys[2], (N,), jnp.float32, -0.9, 0.9))
    return (scale[None, :] * (0.6 * common[None, :] + 0.8 * own)).astype(jnp.float32)


def steps_of(key, extent, pieces, least, top_value):
    factor_of, own = 1.0, jax.random.fold_in(key, 6)
    for dim, shards_of in pieces:
        heights = jnp.exp(jax.random.uniform(jax.random.fold_in(own, dim), (shards_of,), jnp.float32, least / len(pieces), top_value / len(pieces)))
        factor_of = factor_of * jnp.repeat(heights, extent[dim] // shards_of).reshape([-1 if axis == dim else 1 for axis in range(len(extent))])
    return factor_of


def centred(rng, extent, scale, bound, cuts=(), held_as=jnp.bfloat16):
    array = jax.random.normal(rng, extent, jnp.float32) * scale
    if len(cuts) > 0:
        array = steps_of(rng, extent, cuts, -0.22, 0.18) * array
    return jnp.clip(array, min=-bound, max=bound).astype(held_as)


def setup_inputs(seed: int = 0) -> dict:
    key_of = jax.random.split(jax.random.key(seed), 9)
    return {
        "tiles": centred(key_of[0], (DEVICES * CAP, TILE, TILE), 0.08, 0.48, ((0, 512),), jnp.float32),
        "tile_rows": draw_tile_rows(jax.random.fold_in(key_of[8], 71), 0),
        "tile_cols": draw_tile_cols(jax.random.fold_in(key_of[8], 71), 0),
        "tile_count": draw_tile_count(jax.random.fold_in(key_of[8], 71), 0),
        "energy": draw_energy(jax.random.fold_in(key_of[8], 71), 0),
        "basis_block": draw_basis_block(jax.random.fold_in(key_of[8], 71), 0),
        "previous_block": centred(key_of[6], (K, N), 1.0, 6.0, ((1, 512),), jnp.float32),
        "coupling": centred(key_of[7], (K, K), 0.5, 2.5, (), jnp.float32),
    }


HIGH = lax.Precision.HIGHEST

def apply_upper(tiles, tile_rows, tile_cols, tile_count, basis_block):
    total = tiles.shape[0]
    slots = jnp.arange(total, dtype=jnp.int32)
    device = slots // CAP
    row_index = device // N_COL
    col_index = device % N_COL
    live = (slots % CAP < tile_count[device]).astype(jnp.float32)
    row_first = (row_index * N_COL * VEC_DEV + tile_rows * TILE).astype(jnp.int32)
    col_local = (tile_cols * TILE).astype(jnp.int32)
    col_first = ((col_local // VEC_DEV * N_COL + col_index) * VEC_DEV + col_local % VEC_DEV).astype(jnp.int32)
    row_tile = (row_first // TILE).astype(jnp.int32)
    col_tile = (col_first // TILE).astype(jnp.int32)
    count_tiles = N // TILE
    blocked = basis_block.reshape(K, count_tiles, TILE)
    x_cols = blocked[:, col_tile, :]
    x_rows = blocked[:, row_tile, :]
    direct = jnp.einsum('kmj,mij->mki', x_cols, tiles, precision=HIGH) * live[:, None, None]
    flipped = jnp.einsum('kmi,mij->mkj', x_rows, tiles, precision=HIGH) * live[:, None, None]
    summed = jax.ops.segment_sum(direct.reshape(total, K * TILE), row_tile, count_tiles)
    summed = summed + jax.ops.segment_sum(flipped.reshape(total, K * TILE), col_tile, count_tiles)
    return summed.reshape(count_tiles, K, TILE).transpose(1, 0, 2).reshape(K, N)

def reference(tiles, tile_rows, tile_cols, tile_count, energy, basis_block, previous_block, coupling):
    image = apply_upper(tiles, tile_rows, tile_cols, tile_count, basis_block) + energy[None, :] * basis_block
    residual0 = image - jnp.dot(coupling, previous_block, precision=HIGH)
    first = jnp.dot(basis_block, residual0.T, precision=HIGH) / N
    residual1 = residual0 - jnp.dot(first.T, basis_block, precision=HIGH)
    second = jnp.dot(basis_block, residual1.T, precision=HIGH) / N
    residual2 = residual1 - jnp.dot(second.T, basis_block, precision=HIGH)
    alpha = first + second
    gram = jnp.dot(residual2, residual2.T, precision=HIGH) / N
    lower = jnp.linalg.cholesky(gram)
    next_block = lax.linalg.triangular_solve(lower, residual2, left_side=True, lower=True)
    return (next_block, alpha, lower.T)
```

```python
import jax
import jax.numpy as jnp
from jax import lax
from jax.experimental import pallas as pl
from jax.experimental.pallas import tpu as pltpu
from jax.sharding import PartitionSpec as P

MESH = pl.DeviceIdType.MESH
HIGH = lax.Precision.HIGHEST
F32 = jnp.float32
ROWS, COLS, CHIPS = 32, 16, 16
K, SLOTS, TILE, WIDTH = 4, 8, 128, 2048
BLOCKS = WIDTH // TILE
CHUNK = BLOCKS + 1
TOTAL = float(WIDTH * ROWS * COLS)
REACH = {1: CHIPS // 2, -1: CHIPS // 2 - 1}
HOP = 2


def dot(a, b, trans_b=False):
    dims = (((1,), (1 if trans_b else 0,)), ((), ()))
    return lax.dot_general(a, b, dims, precision=HIGH, preferred_element_type=F32)


def two_sum(a, b):
    s = a + b
    t = s - a
    return s, (a - (s - t)) + (b - t)


def split(a):
    c = a * 4097.0
    high = c - (c - a)
    return high, a - high


def two_prod(a, b):
    p = a * b
    ah, al = split(a)
    bh, bl = split(b)
    return p, ((ah * bh - p) + ah * bl + al * bh) + al * bl


def fold_rows(x, e):
    for s in (4, 2, 1):
        x, r = two_sum(x, pltpu.roll(x, s, 0))
        e = e + pltpu.roll(e, s, 0) + r
    return x, e


def sum_pairs(rows):
    x, e = rows[0:8], jnp.zeros((8, TILE), F32)
    for r in range(8, rows.shape[0], 8):
        x, t = two_sum(x, rows[r : r + 8])
        e = e + t
    x, e = fold_rows(x, e)
    lane = lax.broadcasted_iota(jnp.int32, (8, TILE), 1)
    return x + jnp.where(lane >= 64, pltpu.roll(e, 64, 1), 0.0)


def pick(row, base, stride_m, stride_k, stride_l, shift=0):
    src = lax.broadcasted_iota(jnp.int32, (TILE, TILE), 0)
    lane = lax.broadcasted_iota(jnp.int32, (TILE, TILE), 1)
    m, k, l = lane // 16, (lane // 4) % 4, lane % 4
    want = base + shift + stride_m * m + stride_k * k + stride_l * l
    hot = jnp.where((src == want) & (lane < 64), 1.0, 0.0).astype(F32)
    return dot(row, hot)


def fold_m(x, e):
    for s in (32, 16):
        x, r = two_sum(x, pltpu.roll(x, TILE - s, 1))
        e = e + pltpu.roll(e, TILE - s, 1) + r
    return x, e


def body(rows, cols, count, coupling, tiles_hbm, energy_hbm, basis_hbm, prev_hbm,
         next_ref, alpha_ref, beta_ref,
         xcol, xrow, tiles, energy, prev, fsend, fbuf, dsend, dbuf, gather, red1, red2, msg,
         local, xs, xr, hs, hr, ps, pr, fs, fr, gs, gr, ds, dr, as1, ar1, as2, ar2):
    i, j = lax.axis_index("row"), lax.axis_index("col")
    sib = (i + 1 - 2 * lax.rem(i, 2), j)

    def chip(d):
        return (lax.rem(i + 2 * d + ROWS, ROWS), j)

    def plane(d):
        return (i, lax.rem(j + d, COLS))

    def send(src, dst, s, r, dev):
        c = pltpu.make_async_remote_copy(
            src_ref=src, dst_ref=dst, send_sem=s, recv_sem=r, device_id=dev, device_id_type=MESH
        )
        c.start()
        return c

    loads = [
        pltpu.make_async_copy(basis_hbm, xcol.at[pl.ds(i * CHUNK, BLOCKS)], local.at[0]),
        pltpu.make_async_copy(basis_hbm, xrow.at[pl.ds(j * CHUNK, BLOCKS)], local.at[1]),
        pltpu.make_async_copy(tiles_hbm, tiles, local.at[2]),
        pltpu.make_async_copy(energy_hbm, energy, local.at[3]),
        pltpu.make_async_copy(prev_hbm, prev, local.at[4]),
    ]
    for c in loads:
        c.start()

    barrier = pltpu.get_barrier_semaphore()
    near = [chip(s * d) for d in range(1, HOP + 1) for s in (1, -1)] + [sib]
    for dev in near:
        pl.semaphore_signal(barrier, inc=1, device_id=dev, device_id_type=MESH)

    @pl.loop(1, COLS)
    def _(d):
        pl.semaphore_signal(barrier, inc=1, device_id=plane(d), device_id_type=MESH)

    sub = lax.broadcasted_iota(jnp.int32, (K, TILE), 0)
    lane = lax.broadcasted_iota(jnp.int32, (K, TILE), 1)
    places = jnp.zeros((K, TILE), F32)
    for t in range(SLOTS):
        live = jnp.full((K, TILE), t, jnp.int32) < jnp.full((K, TILE), count[0], jnp.int32)
        c = jnp.where(live, jnp.full((K, TILE), cols[t], jnp.int32), -1).astype(F32)
        r = jnp.where(live, jnp.full((K, TILE), rows[t], jnp.int32), -1).astype(F32)
        places = jnp.where((sub == i // 16) & (lane == lax.rem(i, 16) * SLOTS + t), c, places)
        places = jnp.where((sub == 2) & (lane == j * SLOTS + t), r, places)
    xcol[i * CHUNK + BLOCKS] = places
    xrow[j * CHUNK + BLOCKS] = places
    loads[0].wait()
    loads[1].wait()
    pl.semaphore_wait(barrier, len(near) + COLS - 1)

    def place(buf, slot):
        return buf.at[pl.ds(slot * CHUNK, CHUNK)] if buf is xcol or buf is xrow else buf.at[slot]

    def ring(buf, ssem, rsem, copies, base, s):
        at = place(buf, lax.rem(i - 2 * s * base + 2 * ROWS, ROWS))
        for d in range(HOP, 0, -1):
            t = base + d
            if t <= REACH[s]:
                n = 2 * (t - 1) + (s < 0)
                copies[(t, s)] = send(at, at, ssem.at[n], rsem.at[n], chip(s * d))

    def share(buf, ssem, rsem, copies, t, s):
        at = place(buf, lax.rem(i - 2 * s * t + 2 * ROWS, ROWS))
        n = len(copies)
        copies.append(send(at, at, ssem.at[n], rsem.at[n], sib))

    def arrive(buf, sems, ssems, copies, shares, hops):
        for t in hops:
            for s in (1, -1):
                if t <= REACH[s]:
                    copies[(t, s)].wait_recv()
                    if t % HOP == 0:
                        ring(buf, *sems, copies, t, s)
        for t in hops:
            for s in (1, -1):
                if t <= REACH[s]:
                    share(buf, *ssems, shares, t, s)

    def over_plane(src, dst, ssem, rsem):
        @pl.loop(1, COLS)
        def _(d):
            send(src, dst, ssem.at[d], rsem.at[d], plane(d))

    def plane_wait(src, dst, ssem, rsem):
        @pl.loop(1, COLS)
        def _(d):
            c = pltpu.make_async_remote_copy(
                src_ref=src, dst_ref=dst, send_sem=ssem.at[d], recv_sem=rsem.at[d],
                device_id=plane(d), device_id_type=MESH,
            )
            c.wait()

    xc, xh, fc, fh = {}, [], {}, []
    ring(xcol, xs, xr, xc, 0, 1)
    ring(xcol, xs, xr, xc, 0, -1)
    share(xcol, hs, hr, xh, 0, 1)
    own = place(xrow, j)
    over_plane(own, own, ps, pr)

    for c in loads[2:]:
        c.wait()

    arrive(xcol, (xs, xr), (hs, hr), xc, xh, (1, 2))
    plane_wait(own, own, ps, pr)

    for t in range(SLOTS):
        r = rows[t]
        v = xrow[r + lax.shift_right_logical(r, 4)]
        y = dot(v, tiles[t])
        for k in range(K):
            fsend[k, t : t + 1, :] = y[k : k + 1, :]
    fbuf[i] = fsend[...]
    ring(fbuf, fs, fr, fc, 0, 1)
    ring(fbuf, fs, fr, fc, 0, -1)
    share(fbuf, gs, gr, fh, 0, 1)

    arrive(xcol, (xs, xr), (hs, hr), xc, xh, (3, 4))
    arrive(fbuf, (fs, fr), (gs, gr), fc, fh, (1, 2))
    arrive(xcol, (xs, xr), (hs, hr), xc, xh, (5, 6))
    arrive(fbuf, (fs, fr), (gs, gr), fc, fh, (3, 4))
    arrive(xcol, (xs, xr), (hs, hr), xc, xh, (7, 8))
    for c in xh:
        c.wait()

    for t in range(SLOTS):
        r = cols[t]
        v = xcol[r + lax.shift_right_logical(r, 4)]
        y = dot(v, tiles[t], trans_b=True)
        for k in range(K):
            dsend[k, t : t + 1, :] = y[k : k + 1, :]
    dbuf[j] = dsend[...]
    over_plane(dbuf.at[j], dbuf.at[j], ds, dr)
    arrive(fbuf, (fs, fr), (gs, gr), fc, fh, (5, 6))

    at_cols = jnp.zeros((K, TILE), F32)
    for d in range(ROWS):
        at_cols = at_cols + xcol[d * CHUNK + BLOCKS]
    at_rows = jnp.zeros((K, TILE), F32)
    for d in range(COLS):
        at_rows = at_rows + xrow[d * CHUNK + BLOCKS]
    block = lax.broadcasted_iota(jnp.int32, (BLOCKS, TILE), 0)

    def hot(line, first):
        return jnp.where(line.astype(jnp.int32) == block + first * BLOCKS, 1.0, 0.0).astype(F32)

    hot_low = hot(at_cols[0:1, :], i)
    hot_high = hot(at_cols[1:2, :], i)
    hot_row = hot(at_rows[2:3, :], j)

    x = [xcol[pl.ds(i * CHUNK, BLOCKS), k, :] for k in range(K)]
    old = [prev[:, k, :] for k in range(K)]
    res = []
    for k in range(K):
        r = energy[...] * x[k]
        for m in range(K):
            r = r - coupling[k, m] * old[m]
        res.append(r)

    gather[...] = jnp.zeros((TILE, TILE), F32)

    def inner(row, a, b):
        gather[row : row + 1, :] = jnp.sum(a * b, axis=0, keepdims=True)

    for k in range(K):
        for l in range(K):
            inner(4 * k + l, x[k], x[l])

    arrive(fbuf, (fs, fr), (gs, gr), fc, fh, (7, 8))
    for c in fh:
        c.wait()
    for k in range(K):
        low = fbuf[0:16, k].reshape(TILE, TILE)
        high = fbuf[16:32, k].reshape(TILE, TILE)
        res[k] = res[k] + (dot(hot_low, low) + dot(hot_high, high))
    plane_wait(dbuf.at[j], dbuf.at[j], ds, dr)
    for k in range(K):
        res[k] = res[k] + dot(hot_row, dbuf[:, k].reshape(TILE, TILE))

    for k in range(K):
        for l in range(K):
            inner(16 + 4 * k + l, x[k], res[l])
            inner(32 + 4 * k + l, res[k], res[l])
    here = dot(jnp.ones((8, TILE), F32), gather[...], trans_b=True)

    msg[0] = here[0:1]
    red1[j] = here[0:1]

    over_plane(msg.at[0], red1.at[j], as1, ar1)
    plane_wait(msg.at[0], red1.at[j], as1, ar1)
    part = sum_pairs(red1[...].reshape(COLS, TILE))
    msg[1] = part[0:1]
    red2[i] = part[0:1]

    def column(d):
        return pltpu.make_async_remote_copy(
            src_ref=msg.at[1], dst_ref=red2.at[i], send_sem=as2.at[d], recv_sem=ar2.at[d],
            device_id=(lax.rem(i + d, ROWS), j), device_id_type=MESH,
        )

    @pl.loop(1, ROWS)
    def _(d):
        column(d).start()

    @pl.loop(1, ROWS)
    def _(d):
        column(d).wait()

    sums = sum_pairs(red2[...].reshape(ROWS, TILE)) * (1.0 / TOTAL)

    g_km, g_km_low = pick(sums, 0, 1, 4, 0), pick(sums, 0, 1, 4, 0, 64)
    f_ml = pick(sums, 16, 4, 0, 1)
    f_mk, f_mk_low = pick(sums, 16, 4, 1, 0), pick(sums, 16, 4, 1, 0, 64)
    first = pltpu.roll(sums, TILE - 16, 1)
    gf, _ = fold_m(g_km * f_ml, jnp.zeros_like(g_km))
    alpha = first + (first - gf)
    a_ml, a_mk = pick(alpha, 0, 4, 0, 1), pick(alpha, 0, 4, 1, 0)
    p, e = two_prod(g_km, a_ml)
    p, e = fold_m(p, e + g_km_low * a_ml)
    p, r = two_sum(p, -first)
    e = e + r - pltpu.roll(sums, TILE - 80, 1)
    p, e = two_sum(p, e)
    t_ml, t_ml_low = pick(p, 0, 4, 0, 1), pick(e, 0, 4, 0, 1)
    p, e = two_prod(a_mk, t_ml)
    q, r = two_prod(-f_mk, a_ml)
    p, s = two_sum(p, q)
    p, e = fold_m(p, e + r + s + a_mk * t_ml_low - f_mk_low * a_ml)
    p, r = two_sum(p, pltpu.roll(sums, TILE - 32, 1))
    gram = p + (e + r + pltpu.roll(sums, TILE - 96, 1))

    def entry(v, k, l):
        return v[0:1, 4 * k + l : 4 * k + l + 1]

    low = {}
    inv = []
    for k in range(K):
        d = entry(gram, k, k)
        for m in range(k):
            d = d - low[k, m] * low[k, m]
        low[k, k] = jnp.sqrt(d)
        inv.append(1.0 / low[k, k])
        for n in range(k + 1, K):
            v = entry(gram, n, k)
            for m in range(k):
                v = v - low[n, m] * low[k, m]
            low[n, k] = v * inv[k]

    done = []
    for l in range(K):
        r = res[l]
        for k in range(K):
            r = r - entry(alpha, k, l) * x[k]
        for m in range(l):
            r = r - low[l, m] * done[m]
        done.append(r * inv[l])
    for k in range(K):
        next_ref[:, k, :] = done[k]

    row4 = lax.broadcasted_iota(jnp.int32, (K, K), 0)
    col4 = lax.broadcasted_iota(jnp.int32, (K, K), 1)
    a, b = jnp.zeros((K, K), F32), jnp.zeros((K, K), F32)
    for k in range(K):
        for l in range(K):
            a = jnp.where((row4 == k) & (col4 == l), entry(alpha, k, l), a)
            if l >= k:
                b = jnp.where((row4 == k) & (col4 == l), low[l, k], b)
    alpha_ref[...] = a
    beta_ref[...] = b

    for c in list(xc.values()) + list(fc.values()):
        c.wait_send()


def step(tiles, tile_rows, tile_cols, tile_count, energy, basis_block, previous_block, coupling):
    vmem, smem, hbm = (pl.BlockSpec(memory_space=m) for m in (pltpu.VMEM, pltpu.SMEM, pl.ANY))
    dma = pltpu.SemaphoreType.DMA
    def blocked(a):
        return a.reshape(K, BLOCKS, TILE).transpose(1, 0, 2)

    out, alpha, beta = pl.pallas_call(
        body,
        out_shape=(
            jax.ShapeDtypeStruct((BLOCKS, K, TILE), F32),
            jax.ShapeDtypeStruct((K, K), F32),
            jax.ShapeDtypeStruct((K, K), F32),
        ),
        in_specs=[smem] * 4 + [hbm] * 4,
        out_specs=(vmem, vmem, vmem),
        scratch_shapes=[
            pltpu.VMEM((ROWS * CHUNK, K, TILE), F32),
            pltpu.VMEM((COLS * CHUNK, K, TILE), F32),
            pltpu.VMEM((SLOTS, TILE, TILE), F32),
            pltpu.VMEM((BLOCKS, TILE), F32),
            pltpu.VMEM((BLOCKS, K, TILE), F32),
            pltpu.VMEM((K, SLOTS, TILE), F32),
            pltpu.VMEM((ROWS, K, SLOTS, TILE), F32),
            pltpu.VMEM((K, SLOTS, TILE), F32),
            pltpu.VMEM((COLS, K, SLOTS, TILE), F32),
            pltpu.VMEM((TILE, TILE), F32),
            pltpu.VMEM((COLS, 1, TILE), F32),
            pltpu.VMEM((ROWS, 1, TILE), F32),
            pltpu.VMEM((2, 1, TILE), F32),
            dma((5,)),
            dma((CHIPS,)), dma((CHIPS,)), dma((CHIPS,)), dma((CHIPS,)),
            dma((COLS,)), dma((COLS,)),
            dma((CHIPS,)), dma((CHIPS,)), dma((CHIPS,)), dma((CHIPS,)),
            dma((COLS,)), dma((COLS,)),
            dma((COLS,)), dma((COLS,)),
            dma((ROWS,)), dma((ROWS,)),
        ],
        compiler_params=pltpu.CompilerParams(
            collective_id=0, has_side_effects=True, vmem_limit_bytes=56 << 20
        ),
        name="lanczos",
    )(
        tile_rows, tile_cols, tile_count, coupling, tiles, energy.reshape(BLOCKS, TILE),
        blocked(basis_block), blocked(previous_block),
    )
    return out.transpose(1, 0, 2).reshape(K, WIDTH), alpha, beta


def solution(mesh):
    both = ("row", "col")
    return jax.shard_map(
        step,
        mesh=mesh,
        in_specs=(
            P(both, None, None), P(both), P(both), P(both), P(both), P(None, both), P(None, both), P(),
        ),
        out_specs=(P(None, both), P(), P()),
        check_vma=False,
    )
```

```python
import jax
import jax.numpy as jnp
from jax import lax
from jax.experimental import pallas as pl
from jax.experimental.pallas import tpu as pltpu
from jax.sharding import PartitionSpec as P

MESH = pl.DeviceIdType.MESH
HIGH = lax.Precision.HIGHEST
F32 = jnp.float32
ROWS, COLS, CHIPS = 32, 16, 16
K, SLOTS, TILE, WIDTH = 4, 8, 128, 2048
BLOCKS = WIDTH // TILE
CHUNK = BLOCKS + 1
TOTAL = float(WIDTH * ROWS * COLS)
TREE = {
    0: (3, -3, 1, -1),
    3: (6, 4, 2), -3: (-6, -4, -2),
    6: (8, 7, 5), -6: (-7, -5),
}
FIRST, SECOND, THIRD = (1, -1, 3, -3), (2, -2, 4, -4, 6, -6), (5, -5, 7, -7, 8)
RING = {0: 0, 1: 1, 2: 2, 3: 1}
PLANE = sorted(
    ((dx, dy) for dx in range(4) for dy in range(4) if dx or dy), key=lambda p: -RING[p[0]] - RING[p[1]]
)
COLUMN = sorted(range(1, CHIPS), key=lambda d: -min(d, CHIPS - d))


def dot(a, b, trans_b=False):
    dims = (((1,), (1 if trans_b else 0,)), ((), ()))
    return lax.dot_general(a, b, dims, precision=HIGH, preferred_element_type=F32)


def two_sum(a, b):
    s = a + b
    t = s - a
    return s, (a - (s - t)) + (b - t)


def split(a):
    c = a * 4097.0
    high = c - (c - a)
    return high, a - high


def two_prod(a, b):
    p = a * b
    ah, al = split(a)
    bh, bl = split(b)
    return p, ((ah * bh - p) + ah * bl + al * bh) + al * bl


def fold_rows(x, e):
    for s in (4, 2, 1):
        x, r = two_sum(x, pltpu.roll(x, s, 0))
        e = e + pltpu.roll(e, s, 0) + r
    return x, e


def sum_pairs(rows):
    x, e = rows[0:8], jnp.zeros((8, TILE), F32)
    for r in range(8, rows.shape[0], 8):
        x, t = two_sum(x, rows[r : r + 8])
        e = e + t
    x, e = fold_rows(x, e)
    lane = lax.broadcasted_iota(jnp.int32, (8, TILE), 1)
    return x + jnp.where(lane >= 64, pltpu.roll(e, 64, 1), 0.0)


def pick(row, base, stride_m, stride_k, stride_l, shift=0):
    src = lax.broadcasted_iota(jnp.int32, (TILE, TILE), 0)
    lane = lax.broadcasted_iota(jnp.int32, (TILE, TILE), 1)
    m, k, l = lane // 16, (lane // 4) % 4, lane % 4
    want = base + shift + stride_m * m + stride_k * k + stride_l * l
    hot = jnp.where((src == want) & (lane < 64), 1.0, 0.0).astype(F32)
    return dot(row, hot)


def fold_m(x, e):
    for s in (32, 16):
        x, r = two_sum(x, pltpu.roll(x, TILE - s, 1))
        e = e + pltpu.roll(e, TILE - s, 1) + r
    return x, e


def body(rows, cols, count, coupling, tiles_hbm, energy_hbm, basis_hbm, prev_hbm,
         next_ref, alpha_ref, beta_ref,
         xcol, xrow, tiles, energy, prev, fsend, fbuf, dsend, dbuf, gather, red1, red2, msg,
         local, sent, xr, hr, pr, fr, gr, dr, ar1, ar2):
    i, j = lax.axis_index("row"), lax.axis_index("col")
    sib = (i + 1 - 2 * lax.rem(i, 2), j)

    def chip(d, other=False):
        core = lax.rem(i, 2)
        return (2 * lax.rem(i // 2 + d + CHIPS, CHIPS) + (1 - core if other else core), j)

    def plane(p):
        return (i, 4 * lax.rem(j // 4 + p[0], 4) + lax.rem(lax.rem(j, 4) + p[1], 4))

    def copy(src, dst, s, r, dev):
        return pltpu.make_async_remote_copy(
            src_ref=src, dst_ref=dst, send_sem=s, recv_sem=r, device_id=dev, device_id_type=MESH
        )

    def arrived(ref, sem):
        copy(ref, ref, sem, sem, sib).wait_recv()

    def left(ref, sem):
        copy(ref, ref, sem, sem, sib).wait_send()

    loads = [
        pltpu.make_async_copy(basis_hbm, xcol.at[pl.ds(i * CHUNK, BLOCKS)], local.at[0]),
        pltpu.make_async_copy(basis_hbm, xrow.at[pl.ds(j * CHUNK, BLOCKS)], local.at[1]),
        pltpu.make_async_copy(tiles_hbm, tiles, local.at[2]),
        pltpu.make_async_copy(energy_hbm, energy, local.at[3]),
        pltpu.make_async_copy(prev_hbm, prev, local.at[4]),
    ]
    for c in loads:
        c.start()

    barrier = pltpu.get_barrier_semaphore()
    near = [chip(s * d) for d in (3, 2, 1) for s in (1, -1)] + [plane(p) for p in PLANE] + [sib]
    for dev in near:
        pl.semaphore_signal(barrier, inc=1, device_id=dev, device_id_type=MESH)

    sub = lax.broadcasted_iota(jnp.int32, (K, TILE), 0)
    lane = lax.broadcasted_iota(jnp.int32, (K, TILE), 1)
    places = jnp.zeros((K, TILE), F32)
    for t in range(SLOTS):
        live = jnp.full((K, TILE), t, jnp.int32) < jnp.full((K, TILE), count[0], jnp.int32)
        c = jnp.where(live, jnp.full((K, TILE), cols[t], jnp.int32), -1).astype(F32)
        r = jnp.where(live, jnp.full((K, TILE), rows[t], jnp.int32), -1).astype(F32)
        places = jnp.where((sub == i // 16) & (lane == lax.rem(i, 16) * SLOTS + t), c, places)
        places = jnp.where((sub == 2) & (lane == j * SLOTS + t), r, places)
    xcol[i * CHUNK + BLOCKS] = places
    xrow[j * CHUNK + BLOCKS] = places
    loads[0].wait()
    loads[1].wait()
    pl.semaphore_wait(barrier, len(near))

    def place(buf, t):
        slot = lax.rem(i - 2 * t + ROWS, ROWS)
        return buf.at[pl.ds(slot * CHUNK, CHUNK)] if buf is xcol else buf.at[slot]

    def onward(buf, n, rsem, hsem, t):
        at = place(buf, t)
        for u in TREE.get(t, ()):
            copy(at, at, sent.at[n], rsem.at[u + CHIPS // 2 - 1], chip(u - t)).start()
        copy(at, at, sent.at[n + 1], hsem.at[0], sib).start()

    def arrive(buf, n, rsem, hsem, hops):
        for t in hops:
            arrived(place(buf, t), rsem.at[t + CHIPS // 2 - 1])
            onward(buf, n, rsem, hsem, t)

    def over_plane(src, dst, n, rsem):
        for p in PLANE:
            copy(src, dst, sent.at[n], rsem.at[0], plane(p)).start()

    own = xrow.at[pl.ds(j * CHUNK, CHUNK)]
    onward(xcol, 0, xr, hr, 0)
    over_plane(own, own, 4, pr)

    for c in loads[2:]:
        c.wait()

    arrive(xcol, 0, xr, hr, FIRST)
    arrived(xrow.at[pl.ds(0, (COLS - 1) * CHUNK)], pr.at[0])

    for t in range(SLOTS):
        r = rows[t]
        v = xrow[r + lax.shift_right_logical(r, 4)]
        y = dot(v, tiles[t])
        for k in range(K):
            fsend[k, t : t + 1, :] = y[k : k + 1, :]
    fbuf[i] = fsend[...]
    onward(fbuf, 2, fr, gr, 0)

    arrive(xcol, 0, xr, hr, SECOND)
    arrive(fbuf, 2, fr, gr, FIRST)
    arrive(xcol, 0, xr, hr, THIRD)
    arrived(xcol.at[pl.ds(0, ROWS // 2 * CHUNK)], hr.at[0])

    for t in range(SLOTS):
        r = cols[t]
        v = xcol[r + lax.shift_right_logical(r, 4)]
        y = dot(v, tiles[t], trans_b=True)
        for k in range(K):
            dsend[k, t : t + 1, :] = y[k : k + 1, :]
    dbuf[j] = dsend[...]
    over_plane(dbuf.at[j], dbuf.at[j], 5, dr)
    arrive(fbuf, 2, fr, gr, SECOND)

    at_cols = jnp.zeros((K, TILE), F32)
    for d in range(ROWS):
        at_cols = at_cols + xcol[d * CHUNK + BLOCKS]
    at_rows = jnp.zeros((K, TILE), F32)
    for d in range(COLS):
        at_rows = at_rows + xrow[d * CHUNK + BLOCKS]
    block = lax.broadcasted_iota(jnp.int32, (BLOCKS, TILE), 0)

    def hot(line, first):
        return jnp.where(line.astype(jnp.int32) == block + first * BLOCKS, 1.0, 0.0).astype(F32)

    hot_low = hot(at_cols[0:1, :], i)
    hot_high = hot(at_cols[1:2, :], i)
    hot_row = hot(at_rows[2:3, :], j)

    x = [xcol[pl.ds(i * CHUNK, BLOCKS), k, :] for k in range(K)]
    old = [prev[:, k, :] for k in range(K)]
    res = []
    for k in range(K):
        r = energy[...] * x[k]
        for m in range(K):
            r = r - coupling[k, m] * old[m]
        res.append(r)

    gather[...] = jnp.zeros((TILE, TILE), F32)

    def inner(row, a, b):
        gather[row : row + 1, :] = jnp.sum(a * b, axis=0, keepdims=True)

    for k in range(K):
        for l in range(K):
            inner(4 * k + l, x[k], x[l])

    arrive(fbuf, 2, fr, gr, THIRD)
    arrived(fbuf.at[pl.ds(0, ROWS // 2)], gr.at[0])
    for k in range(K):
        low = fbuf[0:16, k].reshape(TILE, TILE)
        high = fbuf[16:32, k].reshape(TILE, TILE)
        res[k] = res[k] + (dot(hot_low, low) + dot(hot_high, high))
    arrived(dbuf.at[pl.ds(0, COLS - 1)], dr.at[0])
    for k in range(K):
        res[k] = res[k] + dot(hot_row, dbuf[:, k].reshape(TILE, TILE))

    for k in range(K):
        for l in range(K):
            inner(16 + 4 * k + l, x[k], res[l])
            inner(32 + 4 * k + l, res[k], res[l])
    here = dot(jnp.ones((8, TILE), F32), gather[...], trans_b=True)

    msg[0] = here[0:1]
    red1[j] = here[0:1]

    over_plane(msg.at[0], red1.at[j], 6, ar1)
    arrived(red1.at[pl.ds(0, COLS - 1)], ar1.at[0])
    part = sum_pairs(red1[...].reshape(COLS, TILE))
    msg[1] = part[0:1]
    red2[i] = part[0:1]

    for d in COLUMN:
        for other in (False, True):
            copy(msg.at[1], red2.at[i], sent.at[7], ar2.at[0], chip(d, other)).start()
    copy(msg.at[1], red2.at[i], sent.at[7], ar2.at[0], sib).start()
    arrived(red2.at[pl.ds(0, ROWS - 1)], ar2.at[0])

    sums = sum_pairs(red2[...].reshape(ROWS, TILE)) * (1.0 / TOTAL)

    g_km, g_km_low = pick(sums, 0, 1, 4, 0), pick(sums, 0, 1, 4, 0, 64)
    f_ml = pick(sums, 16, 4, 0, 1)
    f_mk, f_mk_low = pick(sums, 16, 4, 1, 0), pick(sums, 16, 4, 1, 0, 64)
    first = pltpu.roll(sums, TILE - 16, 1)
    gf, _ = fold_m(g_km * f_ml, jnp.zeros_like(g_km))
    alpha = first + (first - gf)
    a_ml, a_mk = pick(alpha, 0, 4, 0, 1), pick(alpha, 0, 4, 1, 0)
    p, e = two_prod(g_km, a_ml)
    p, e = fold_m(p, e + g_km_low * a_ml)
    p, r = two_sum(p, -first)
    e = e + r - pltpu.roll(sums, TILE - 80, 1)
    p, e = two_sum(p, e)
    t_ml, t_ml_low = pick(p, 0, 4, 0, 1), pick(e, 0, 4, 0, 1)
    p, e = two_prod(a_mk, t_ml)
    q, r = two_prod(-f_mk, a_ml)
    p, s = two_sum(p, q)
    p, e = fold_m(p, e + r + s + a_mk * t_ml_low - f_mk_low * a_ml)
    p, r = two_sum(p, pltpu.roll(sums, TILE - 32, 1))
    gram = p + (e + r + pltpu.roll(sums, TILE - 96, 1))

    def entry(v, k, l):
        return v[0:1, 4 * k + l : 4 * k + l + 1]

    low = {}
    inv = []
    for k in range(K):
        d = entry(gram, k, k)
        for m in range(k):
            d = d - low[k, m] * low[k, m]
        low[k, k] = jnp.sqrt(d)
        inv.append(1.0 / low[k, k])
        for n in range(k + 1, K):
            v = entry(gram, n, k)
            for m in range(k):
                v = v - low[n, m] * low[k, m]
            low[n, k] = v * inv[k]

    done = []
    for l in range(K):
        r = res[l]
        for k in range(K):
            r = r - entry(alpha, k, l) * x[k]
        for m in range(l):
            r = r - low[l, m] * done[m]
        done.append(r * inv[l])
    for k in range(K):
        next_ref[:, k, :] = done[k]

    row4 = lax.broadcasted_iota(jnp.int32, (K, K), 0)
    col4 = lax.broadcasted_iota(jnp.int32, (K, K), 1)
    a, b = jnp.zeros((K, K), F32), jnp.zeros((K, K), F32)
    for k in range(K):
        for l in range(K):
            a = jnp.where((row4 == k) & (col4 == l), entry(alpha, k, l), a)
            if l >= k:
                b = jnp.where((row4 == k) & (col4 == l), low[l, k], b)
    alpha_ref[...] = a
    beta_ref[...] = b

    left(xcol.at[pl.ds(0, (CHIPS - 1) * CHUNK)], sent.at[0])
    left(xcol.at[pl.ds(0, CHIPS * CHUNK)], sent.at[1])
    left(fbuf.at[pl.ds(0, CHIPS - 1)], sent.at[2])
    left(fbuf.at[pl.ds(0, CHIPS)], sent.at[3])
    left(xrow.at[pl.ds(0, (COLS - 1) * CHUNK)], sent.at[4])
    left(dbuf.at[pl.ds(0, COLS - 1)], sent.at[5])
    left(red1.at[pl.ds(0, COLS - 1)], sent.at[6])
    left(red2.at[pl.ds(0, ROWS - 1)], sent.at[7])


def hand_over(*refs):
    n = len(refs) // 2
    sems = refs[-1]
    copies = [pltpu.make_async_copy(refs[k], refs[n + k], sems.at[k]) for k in range(n)]
    for c in copies:
        c.start()
    for c in copies:
        c.wait()


def step(tiles, tile_rows, tile_cols, tile_count, energy, basis_block, previous_block, coupling):
    vmem, smem, hbm = (pl.BlockSpec(memory_space=m) for m in (pltpu.VMEM, pltpu.SMEM, pl.ANY))
    dma = pltpu.SemaphoreType.DMA
    def blocked(a):
        return a.reshape(K, BLOCKS, TILE).transpose(1, 0, 2)

    out, alpha, beta = pl.pallas_call(
        body,
        out_shape=(
            jax.ShapeDtypeStruct((BLOCKS, K, TILE), F32),
            jax.ShapeDtypeStruct((K, K), F32),
            jax.ShapeDtypeStruct((K, K), F32),
        ),
        in_specs=[smem] * 4 + [hbm] * 4,
        out_specs=(vmem, vmem, vmem),
        scratch_shapes=[
            pltpu.VMEM((ROWS * CHUNK, K, TILE), F32),
            pltpu.VMEM((COLS * CHUNK, K, TILE), F32),
            pltpu.VMEM((SLOTS, TILE, TILE), F32),
            pltpu.VMEM((BLOCKS, TILE), F32),
            pltpu.VMEM((BLOCKS, K, TILE), F32),
            pltpu.VMEM((K, SLOTS, TILE), F32),
            pltpu.VMEM((ROWS, K, SLOTS, TILE), F32),
            pltpu.VMEM((K, SLOTS, TILE), F32),
            pltpu.VMEM((COLS, K, SLOTS, TILE), F32),
            pltpu.VMEM((TILE, TILE), F32),
            pltpu.VMEM((COLS, 1, TILE), F32),
            pltpu.VMEM((ROWS, 1, TILE), F32),
            pltpu.VMEM((2, 1, TILE), F32),
            dma((5,)),
            dma((8,)),
            dma((CHIPS,)), dma((1,)), dma((1,)),
            dma((CHIPS,)), dma((1,)), dma((1,)),
            dma((1,)), dma((1,)),
        ],
        compiler_params=pltpu.CompilerParams(
            collective_id=0, has_side_effects=True, vmem_limit_bytes=56 << 20
        ),
        name="lanczos",
    )(
        tile_rows, tile_cols, tile_count, coupling, tiles, energy.reshape(BLOCKS, TILE),
        blocked(basis_block), blocked(previous_block),
    )
    results = (out, alpha, beta)
    out, alpha, beta = pl.pallas_call(
        hand_over,
        out_shape=tuple(jax.ShapeDtypeStruct(r.shape, F32) for r in results),
        in_specs=[hbm] * 3,
        out_specs=(hbm,) * 3,
        scratch_shapes=[dma((3,))],
        compiler_params=pltpu.CompilerParams(vmem_limit_bytes=56 << 20),
        name="hand_over",
    )(*results)
    return out.transpose(1, 0, 2).reshape(K, WIDTH), alpha, beta


def solution(mesh):
    both = ("row", "col")
    return jax.shard_map(
        step,
        mesh=mesh,
        in_specs=(
            P(both, None, None), P(both), P(both), P(both), P(both), P(None, both), P(None, both), P(),
        ),
        out_specs=(P(None, both), P(), P()),
        check_vma=False,
    )
```

```python
import jax
import jax.numpy as jnp
from jax import lax
from jax.experimental import pallas as pl
from jax.experimental.pallas import tpu as pltpu
from jax.sharding import PartitionSpec as P

MESH = pl.DeviceIdType.MESH
HIGH = lax.Precision.HIGHEST
F32 = jnp.float32
ROWS, COLS, CHIPS = 32, 16, 16
K, SLOTS, TILE, WIDTH = 4, 8, 128, 2048
BLOCKS = WIDTH // TILE
CHUNK = BLOCKS + 1
TOTAL = float(WIDTH * ROWS * COLS)
TREE = {
    0: (3, -3, 1, -1),
    3: (6, 4, 2), -3: (-6, -4, -2),
    6: (8, 7, 5), -6: (-7, -5),
}
FIRST, SECOND, THIRD = (1, -1, 3, -3), (2, -2, 4, -4, 6, -6), (5, -5, 7, -7, 8)
RING = {0: 0, 1: 1, 2: 2, 3: 1}
PLANE = sorted(
    ((dx, dy) for dx in range(4) for dy in range(4) if dx or dy), key=lambda p: -RING[p[0]] - RING[p[1]]
)
COLUMN = sorted(range(1, CHIPS), key=lambda d: -min(d, CHIPS - d))


def dot(a, b, trans_b=False):
    dims = (((1,), (1 if trans_b else 0,)), ((), ()))
    return lax.dot_general(a, b, dims, precision=HIGH, preferred_element_type=F32)


def thirds(a):
    parts = []
    for _ in range(3):
        p = a.astype(jnp.bfloat16).astype(F32)
        parts.append(p)
        a = a - p
    return parts


def split_tile(tile, out):
    for n, p in enumerate(thirds(tile)):
        out[n * TILE : (n + 1) * TILE, :] = p.astype(jnp.bfloat16)


def product(x, tile):
    left = jnp.concatenate(thirds(x) + [jnp.zeros_like(x)], axis=0).astype(jnp.bfloat16)
    y = lax.dot_general(
        jnp.concatenate([left] * 3, axis=1), tile, (((1,), (0,)), ((), ())), preferred_element_type=F32
    )
    return (y[8:12] + y[4:8]) + y[0:4]


def two_sum(a, b):
    s = a + b
    t = s - a
    return s, (a - (s - t)) + (b - t)


def split(a):
    c = a * 4097.0
    high = c - (c - a)
    return high, a - high


def two_prod(a, b):
    p = a * b
    ah, al = split(a)
    bh, bl = split(b)
    return p, ((ah * bh - p) + ah * bl + al * bh) + al * bl


def fold_rows(x, e):
    for s in (4, 2, 1):
        x, r = two_sum(x, pltpu.roll(x, s, 0))
        e = e + pltpu.roll(e, s, 0) + r
    return x, e


def sum_pairs(rows):
    x, e = rows[0:8], jnp.zeros((8, TILE), F32)
    for r in range(8, rows.shape[0], 8):
        x, t = two_sum(x, rows[r : r + 8])
        e = e + t
    x, e = fold_rows(x, e)
    lane = lax.broadcasted_iota(jnp.int32, (8, TILE), 1)
    return x + jnp.where(lane >= 64, pltpu.roll(e, 64, 1), 0.0)


def pick(row, base, stride_m, stride_k, stride_l):
    lane = lax.broadcasted_iota(jnp.int32, (8, TILE), 1)
    m, k, l = lane // 16 % 4, lane // 4 % 4, lane % 4
    src = base + stride_m * m + stride_k * k + stride_l * l
    return jnp.take_along_axis(row, src, axis=1, mode="promise_in_bounds")


def fold_m(x, e):
    for s in (32, 16):
        x, r = two_sum(x, pltpu.roll(x, TILE - s, 1))
        e = e + pltpu.roll(e, TILE - s, 1) + r
    return x, e


def body(count, rows_hbm, cols_hbm, coupling_hbm, tiles_hbm, energy_hbm, basis_hbm, prev_hbm,
         next_ref, alpha_ref, beta_ref,
         rows, cols, coupling, xcol, xrow, tiles, parts, flipped, energy, prev, fsend, fbuf, dsend, dbuf, gather, red1, red2, msg,
         local, sent, xr, hr, pr, fr, gr, dr, ar1, ar2):
    i, j = lax.axis_index("row"), lax.axis_index("col")
    sib = (i + 1 - 2 * lax.rem(i, 2), j)

    def chip(d, other=False):
        core = lax.rem(i, 2)
        return (2 * lax.rem(i // 2 + d + CHIPS, CHIPS) + (1 - core if other else core), j)

    def plane(p):
        return (i, 4 * lax.rem(j // 4 + p[0], 4) + lax.rem(lax.rem(j, 4) + p[1], 4))

    def copy(src, dst, s, r, dev):
        return pltpu.make_async_remote_copy(
            src_ref=src, dst_ref=dst, send_sem=s, recv_sem=r, device_id=dev, device_id_type=MESH
        )

    def arrived(ref, sem):
        copy(ref, ref, sem, sem, sib).wait_recv()

    def left(ref, sem):
        copy(ref, ref, sem, sem, sib).wait_send()

    loads = [
        pltpu.make_async_copy(basis_hbm, xcol.at[pl.ds(i * CHUNK, BLOCKS)], local.at[0]),
        pltpu.make_async_copy(basis_hbm, xrow.at[pl.ds(j * CHUNK, BLOCKS)], local.at[1]),
        pltpu.make_async_copy(tiles_hbm, tiles, local.at[2]),
        pltpu.make_async_copy(energy_hbm, energy, local.at[3]),
        pltpu.make_async_copy(prev_hbm, prev, local.at[4]),
        pltpu.make_async_copy(rows_hbm, rows, local.at[5]),
        pltpu.make_async_copy(cols_hbm, cols, local.at[6]),
        pltpu.make_async_copy(coupling_hbm, coupling, local.at[7]),
    ]
    for c in loads:
        c.start()

    barrier = pltpu.get_barrier_semaphore()
    near = [chip(s * d) for d in (3, 2, 1) for s in (1, -1)] + [plane(p) for p in PLANE] + [sib]
    for dev in near:
        pl.semaphore_signal(barrier, inc=1, device_id=dev, device_id_type=MESH)

    for c in loads[5:]:
        c.wait()

    sub = lax.broadcasted_iota(jnp.int32, (K, TILE), 0)
    lane = lax.broadcasted_iota(jnp.int32, (K, TILE), 1)
    places = jnp.zeros((K, TILE), F32)
    for t in range(SLOTS):
        live = jnp.full((K, TILE), t, jnp.int32) < jnp.full((K, TILE), count[0], jnp.int32)
        c = jnp.where(live, jnp.full((K, TILE), cols[t], jnp.int32), -1).astype(F32)
        r = jnp.where(live, jnp.full((K, TILE), rows[t], jnp.int32), -1).astype(F32)
        places = jnp.where((sub == i // 16) & (lane == lax.rem(i, 16) * SLOTS + t), c, places)
        places = jnp.where((sub == 2) & (lane == j * SLOTS + t), r, places)
    xcol[i * CHUNK + BLOCKS] = places
    xrow[j * CHUNK + BLOCKS] = places
    loads[0].wait()
    loads[1].wait()
    pl.semaphore_wait(barrier, len(near))

    def place(buf, t):
        slot = lax.rem(i - 2 * t + ROWS, ROWS)
        return buf.at[pl.ds(slot * CHUNK, CHUNK)] if buf is xcol else buf.at[slot]

    def onward(buf, n, rsem, hsem, t):
        at = place(buf, t)
        for u in TREE.get(t, ()):
            copy(at, at, sent.at[n], rsem.at[u + CHIPS // 2 - 1], chip(u - t)).start()
        copy(at, at, sent.at[n + 1], hsem.at[0], sib).start()

    def arrive(buf, n, rsem, hsem, hops):
        for t in hops:
            arrived(place(buf, t), rsem.at[t + CHIPS // 2 - 1])
            onward(buf, n, rsem, hsem, t)

    def over_plane(src, dst, n, rsem):
        for p in PLANE:
            copy(src, dst, sent.at[n], rsem.at[0], plane(p)).start()

    own = xrow.at[pl.ds(j * CHUNK, CHUNK)]
    onward(xcol, 0, xr, hr, 0)
    over_plane(own, own, 4, pr)

    for c in loads[2:5]:
        c.wait()
    for t in range(SLOTS):
        split_tile(tiles[t], parts.at[t])

    arrive(xcol, 0, xr, hr, FIRST)
    arrived(xrow.at[pl.ds(0, (COLS - 1) * CHUNK)], pr.at[0])

    for t in range(SLOTS):
        r = rows[t]
        v = xrow[r + lax.shift_right_logical(r, 4)]
        y = product(v, parts[t])
        for k in range(K):
            fsend[k, t : t + 1, :] = y[k : k + 1, :]
    fbuf[i] = fsend[...]
    onward(fbuf, 2, fr, gr, 0)
    for t in range(SLOTS):
        split_tile(tiles[t].T, flipped.at[t])

    arrive(xcol, 0, xr, hr, SECOND)
    arrive(fbuf, 2, fr, gr, FIRST)
    arrive(xcol, 0, xr, hr, THIRD)
    arrive(fbuf, 2, fr, gr, SECOND)
    arrived(xcol.at[pl.ds(0, ROWS // 2 * CHUNK)], hr.at[0])

    for t in range(SLOTS):
        r = cols[t]
        v = xcol[r + lax.shift_right_logical(r, 4)]
        y = product(v, flipped[t])
        for k in range(K):
            dsend[k, t : t + 1, :] = y[k : k + 1, :]
    dbuf[j] = dsend[...]
    over_plane(dbuf.at[j], dbuf.at[j], 5, dr)

    at_cols = jnp.zeros((K, TILE), F32)
    for d in range(ROWS):
        at_cols = at_cols + xcol[d * CHUNK + BLOCKS]
    at_rows = jnp.zeros((K, TILE), F32)
    for d in range(COLS):
        at_rows = at_rows + xrow[d * CHUNK + BLOCKS]
    block = lax.broadcasted_iota(jnp.int32, (BLOCKS, TILE), 0)

    def hot(line, first):
        return jnp.where(line.astype(jnp.int32) == block + first * BLOCKS, 1.0, 0.0).astype(F32)

    hot_low = hot(at_cols[0:1, :], i)
    hot_high = hot(at_cols[1:2, :], i)
    hot_row = hot(at_rows[2:3, :], j)

    x = [xcol[pl.ds(i * CHUNK, BLOCKS), k, :] for k in range(K)]
    old = [prev[:, k, :] for k in range(K)]
    res = []
    for k in range(K):
        r = energy[...] * x[k]
        for m in range(K):
            r = r - coupling[k, m] * old[m]
        res.append(r)

    gather[...] = jnp.zeros((TILE, TILE), F32)

    def inner(row, a, b):
        gather[row : row + 1, :] = jnp.sum(a * b, axis=0, keepdims=True)

    for k in range(K):
        for l in range(K):
            inner(4 * k + l, x[k], x[l])

    arrive(fbuf, 2, fr, gr, THIRD)
    arrived(fbuf.at[pl.ds(0, ROWS // 2)], gr.at[0])
    for k in range(K):
        low = fbuf[0:16, k].reshape(TILE, TILE)
        high = fbuf[16:32, k].reshape(TILE, TILE)
        res[k] = res[k] + (dot(hot_low, low) + dot(hot_high, high))
    arrived(dbuf.at[pl.ds(0, COLS - 1)], dr.at[0])
    for k in range(K):
        res[k] = res[k] + dot(hot_row, dbuf[:, k].reshape(TILE, TILE))

    for k in range(K):
        for l in range(K):
            inner(16 + 4 * k + l, x[k], res[l])
            inner(32 + 4 * k + l, res[k], res[l])
    here = dot(jnp.ones((8, TILE), F32), gather[...], trans_b=True)

    msg[0] = here[0:1]
    red1[j] = here[0:1]

    over_plane(msg.at[0], red1.at[j], 6, ar1)
    arrived(red1.at[pl.ds(0, COLS - 1)], ar1.at[0])
    part = sum_pairs(red1[...].reshape(COLS, TILE))
    msg[1] = part[0:1]
    red2[i] = part[0:1]

    for d in COLUMN:
        for other in (False, True):
            copy(msg.at[1], red2.at[i], sent.at[7], ar2.at[0], chip(d, other)).start()
    copy(msg.at[1], red2.at[i], sent.at[7], ar2.at[0], sib).start()
    arrived(red2.at[pl.ds(0, ROWS - 1)], ar2.at[0])

    sums = sum_pairs(red2[...].reshape(ROWS, TILE)) * (1.0 / TOTAL)

    g_km, g_km_low = pick(sums, 0, 1, 4, 0), pick(sums, 64, 1, 4, 0)
    f_ml = pick(sums, 16, 4, 0, 1)
    f_mk, f_mk_low = pick(sums, 16, 4, 1, 0), pick(sums, 80, 4, 1, 0)
    first = pltpu.roll(sums, TILE - 16, 1)
    gf, _ = fold_m(g_km * f_ml, jnp.zeros_like(g_km))
    alpha = first + (first - gf)
    a_ml, a_mk = pick(alpha, 0, 4, 0, 1), pick(alpha, 0, 4, 1, 0)
    p, e = two_prod(g_km, a_ml)
    p, e = fold_m(p, e + g_km_low * a_ml)
    p, r = two_sum(p, -first)
    e = e + r - pltpu.roll(sums, TILE - 80, 1)
    p, e = two_sum(p, e)
    t_ml, t_ml_low = pick(p, 0, 4, 0, 1), pick(e, 0, 4, 0, 1)
    p, e = two_prod(a_mk, t_ml)
    q, r = two_prod(-f_mk, a_ml)
    p, s = two_sum(p, q)
    p, e = fold_m(p, e + r + s + a_mk * t_ml_low - f_mk_low * a_ml)
    p, r = two_sum(p, pltpu.roll(sums, TILE - 32, 1))
    gram = p + (e + r + pltpu.roll(sums, TILE - 96, 1))

    def entry(v, k, l):
        return v[0:1, 4 * k + l : 4 * k + l + 1]

    low = {}
    inv = []
    for k in range(K):
        d = entry(gram, k, k)
        for m in range(k):
            d = d - low[k, m] * low[k, m]
        low[k, k] = jnp.sqrt(d)
        inv.append(1.0 / low[k, k])
        for n in range(k + 1, K):
            v = entry(gram, n, k)
            for m in range(k):
                v = v - low[n, m] * low[k, m]
            low[n, k] = v * inv[k]

    done = []
    for l in range(K):
        r = res[l]
        for k in range(K):
            r = r - entry(alpha, k, l) * x[k]
        for m in range(l):
            r = r - low[l, m] * done[m]
        done.append(r * inv[l])
    for k in range(K):
        next_ref[:, k, :] = done[k]

    row4 = lax.broadcasted_iota(jnp.int32, (K, K), 0)
    col4 = lax.broadcasted_iota(jnp.int32, (K, K), 1)
    a, b = jnp.zeros((K, K), F32), jnp.zeros((K, K), F32)
    for k in range(K):
        for l in range(K):
            a = jnp.where((row4 == k) & (col4 == l), entry(alpha, k, l), a)
            if l >= k:
                b = jnp.where((row4 == k) & (col4 == l), low[l, k], b)
    alpha_ref[...] = a
    beta_ref[...] = b

    left(xcol.at[pl.ds(0, (CHIPS - 1) * CHUNK)], sent.at[0])
    left(xcol.at[pl.ds(0, CHIPS * CHUNK)], sent.at[1])
    left(fbuf.at[pl.ds(0, CHIPS - 1)], sent.at[2])
    left(fbuf.at[pl.ds(0, CHIPS)], sent.at[3])
    left(xrow.at[pl.ds(0, (COLS - 1) * CHUNK)], sent.at[4])
    left(dbuf.at[pl.ds(0, COLS - 1)], sent.at[5])
    left(red1.at[pl.ds(0, COLS - 1)], sent.at[6])
    left(red2.at[pl.ds(0, ROWS - 1)], sent.at[7])


def hand_over(*refs):
    n = len(refs) // 2
    sems = refs[-1]
    copies = [pltpu.make_async_copy(refs[k], refs[n + k], sems.at[k]) for k in range(n)]
    for c in copies:
        c.start()
    for c in copies:
        c.wait()


def step(tiles, tile_rows, tile_cols, tile_count, energy, basis_block, previous_block, coupling):
    vmem, hbm = (pl.BlockSpec(memory_space=m) for m in (pltpu.VMEM, pl.ANY))
    dma = pltpu.SemaphoreType.DMA
    def blocked(a):
        return a.reshape(K, BLOCKS, TILE).transpose(1, 0, 2)

    operands = (
        tile_rows, tile_cols, coupling, tiles, energy.reshape(BLOCKS, TILE),
        blocked(basis_block), blocked(previous_block),
    )
    out, alpha, beta = pl.pallas_call(
        body,
        out_shape=(
            pltpu.VMEM((BLOCKS, K, TILE), F32),
            pltpu.VMEM((K, K), F32),
            pltpu.VMEM((K, K), F32),
        ),
        in_specs=[pl.BlockSpec(memory_space=pltpu.SMEM)] + [hbm] * 7,
        out_specs=(vmem, vmem, vmem),
        scratch_shapes=[
            pltpu.SMEM((SLOTS,), jnp.int32),
            pltpu.SMEM((SLOTS,), jnp.int32),
            pltpu.SMEM((K, K), F32),
            pltpu.VMEM((ROWS * CHUNK, K, TILE), F32),
            pltpu.VMEM((COLS * CHUNK, K, TILE), F32),
            pltpu.VMEM((SLOTS, TILE, TILE), F32),
            pltpu.VMEM((SLOTS, 3 * TILE, TILE), jnp.bfloat16),
            pltpu.VMEM((SLOTS, 3 * TILE, TILE), jnp.bfloat16),
            pltpu.VMEM((BLOCKS, TILE), F32),
            pltpu.VMEM((BLOCKS, K, TILE), F32),
            pltpu.VMEM((K, SLOTS, TILE), F32),
            pltpu.VMEM((ROWS, K, SLOTS, TILE), F32),
            pltpu.VMEM((K, SLOTS, TILE), F32),
            pltpu.VMEM((COLS, K, SLOTS, TILE), F32),
            pltpu.VMEM((TILE, TILE), F32),
            pltpu.VMEM((COLS, 1, TILE), F32),
            pltpu.VMEM((ROWS, 1, TILE), F32),
            pltpu.VMEM((2, 1, TILE), F32),
            dma((8,)),
            dma((8,)),
            dma((CHIPS,)), dma((1,)), dma((1,)),
            dma((CHIPS,)), dma((1,)), dma((1,)),
            dma((1,)), dma((1,)),
        ],
        compiler_params=pltpu.CompilerParams(
            collective_id=0, has_side_effects=True, vmem_limit_bytes=32 << 20
        ),
        name="lanczos",
    )(tile_count, *(pltpu.with_memory_space_constraint(a, pltpu.HBM) for a in operands))
    results = (out, alpha, beta)
    out, alpha, beta = pl.pallas_call(
        hand_over,
        out_shape=tuple(jax.ShapeDtypeStruct(r.shape, F32) for r in results),
        in_specs=[hbm] * 3,
        out_specs=(hbm,) * 3,
        scratch_shapes=[dma((3,))],
        compiler_params=pltpu.CompilerParams(vmem_limit_bytes=1 << 20),
        name="hand_over",
    )(*results)
    return out.transpose(1, 0, 2).reshape(K, WIDTH), alpha, beta


def solution(mesh):
    both = ("row", "col")
    return jax.shard_map(
        step,
        mesh=mesh,
        in_specs=(
            P(both, None, None), P(both), P(both), P(both), P(both), P(None, both), P(None, both), P(),
        ),
        out_specs=(P(None, both), P(), P()),
        check_vma=False,
    )
```

```python
import jax
import jax.numpy as jnp
from jax import lax
from jax.experimental import pallas as pl
from jax.experimental.pallas import tpu as pltpu
from jax.sharding import PartitionSpec as P

MESH = pl.DeviceIdType.MESH
HIGH = lax.Precision.HIGHEST
F32 = jnp.float32
ROWS, COLS, CHIPS = 32, 16, 16
K, SLOTS, TILE, WIDTH = 4, 8, 128, 2048
BLOCKS = WIDTH // TILE
CHUNK = BLOCKS + 1
TOTAL = float(WIDTH * ROWS * COLS)
TREE = {
    0: (3, -3, 1, -1),
    3: (6, 4, 2), -3: (-6, -4, -2),
    6: (8, 7, 5), -6: (-7, -5),
}
WAVES = (1, -1, 3, -3), (2, -2, 4, -4, 6, -6), (5, -5, 7, -7, 8)
LIST_TREE = {0: (3, -3, 1, -1), 3: (6, 4, 2), -3: (-6, -4, -2), 6: (8, 7, 5), -6: (-7, -5)}
LIST_WAVES = ((1, -1, 3, -3), (2, -2, 4, -4, 6, -6), (5, -5, 7, -7, 8))
RING = {0: 0, 1: 1, 2: 2, 3: 1}
PLANE = sorted(
    ((dx, dy) for dx in range(4) for dy in range(4) if dx or dy), key=lambda p: -RING[p[0]] - RING[p[1]]
)
COLUMN = sorted(range(1, CHIPS), key=lambda d: -min(d, CHIPS - d))


def dot(a, b, trans_b=False):
    dims = (((1,), (1 if trans_b else 0,)), ((), ()))
    return lax.dot_general(a, b, dims, precision=HIGH, preferred_element_type=F32)


def thirds(a):
    parts = []
    for _ in range(3):
        p = a.astype(jnp.bfloat16).astype(F32)
        parts.append(p)
        a = a - p
    return parts


def split_tile(tile, out):
    for n, p in enumerate(thirds(tile)):
        out[n * TILE : (n + 1) * TILE, :] = p.astype(jnp.bfloat16)


def product(x, tile):
    left = jnp.concatenate(thirds(x) + [jnp.zeros_like(x)], axis=0).astype(jnp.bfloat16)
    y = lax.dot_general(
        jnp.concatenate([left] * 3, axis=1), tile, (((1,), (0,)), ((), ())), preferred_element_type=F32
    )
    return (y[8:12] + y[4:8]) + y[0:4]


def two_sum(a, b):
    s = a + b
    t = s - a
    return s, (a - (s - t)) + (b - t)


def split(a):
    c = a * 4097.0
    high = c - (c - a)
    return high, a - high


def two_prod(a, b):
    p = a * b
    ah, al = split(a)
    bh, bl = split(b)
    return p, ((ah * bh - p) + ah * bl + al * bh) + al * bl


def fold_rows(x, e):
    for s in (4, 2, 1):
        x, r = two_sum(x, pltpu.roll(x, s, 0))
        e = e + pltpu.roll(e, s, 0) + r
    return x, e


def sum_pairs(rows):
    x, e = rows[0:8], jnp.zeros((8, TILE), F32)
    for r in range(8, rows.shape[0], 8):
        x, t = two_sum(x, rows[r : r + 8])
        e = e + t
    x, e = fold_rows(x, e)
    lane = lax.broadcasted_iota(jnp.int32, (8, TILE), 1)
    return x + jnp.where(lane >= 64, pltpu.roll(e, 64, 1), 0.0)


def pick(row, base, stride_m, stride_k, stride_l):
    lane = lax.broadcasted_iota(jnp.int32, (8, TILE), 1)
    m, k, l = lane // 16 % 4, lane // 4 % 4, lane % 4
    src = base + stride_m * m + stride_k * k + stride_l * l
    return jnp.take_along_axis(row, src, axis=1, mode="promise_in_bounds")


def fold_m(x, e):
    for s in (32, 16):
        x, r = two_sum(x, pltpu.roll(x, TILE - s, 1))
        e = e + pltpu.roll(e, TILE - s, 1) + r
    return x, e


def body(count, rows_hbm, cols_hbm, coupling_hbm, tiles_hbm, energy_hbm, basis_hbm, prev_hbm,
         next_ref, alpha_ref, beta_ref,
         rows, cols, coupling, xcol, xrow, tiles, parts, flipped, energy, prev, fsend, fbuf, dsend, dbuf, gather, red1, red2, msg,
         local, sent, xr, hr, pr, fr, gr, dr, ar1, ar2):
    i, j = lax.axis_index("row"), lax.axis_index("col")
    sib = (i + 1 - 2 * lax.rem(i, 2), j)

    def chip(d, other=False):
        core = lax.rem(i, 2)
        return (2 * lax.rem(i // 2 + d + CHIPS, CHIPS) + (1 - core if other else core), j)

    def plane(p):
        return (i, 4 * lax.rem(j // 4 + p[0], 4) + lax.rem(lax.rem(j, 4) + p[1], 4))

    def copy(src, dst, s, r, dev):
        return pltpu.make_async_remote_copy(
            src_ref=src, dst_ref=dst, send_sem=s, recv_sem=r, device_id=dev, device_id_type=MESH
        )

    def arrived(ref, sem):
        copy(ref, ref, sem, sem, sib).wait_recv()

    def left(ref, sem):
        copy(ref, ref, sem, sem, sib).wait_send()

    loads = [
        pltpu.make_async_copy(basis_hbm, xcol.at[pl.ds(i * CHUNK, BLOCKS)], local.at[0]),
        pltpu.make_async_copy(basis_hbm, xrow.at[pl.ds(j * CHUNK, BLOCKS)], local.at[1]),
        pltpu.make_async_copy(tiles_hbm, tiles, local.at[2]),
        pltpu.make_async_copy(energy_hbm, energy, local.at[3]),
        pltpu.make_async_copy(prev_hbm, prev, local.at[4]),
        pltpu.make_async_copy(rows_hbm, rows, local.at[5]),
        pltpu.make_async_copy(cols_hbm, cols, local.at[6]),
        pltpu.make_async_copy(coupling_hbm, coupling, local.at[7]),
    ]
    for c in loads:
        c.start()

    barrier = pltpu.get_barrier_semaphore()
    near = [chip(s * d) for d in (3, 2, 1) for s in (1, -1)] + [plane(p) for p in PLANE] + [sib]
    for dev in near:
        pl.semaphore_signal(barrier, inc=1, device_id=dev, device_id_type=MESH)

    for c in loads[5:]:
        c.wait()

    sub = lax.broadcasted_iota(jnp.int32, (K, TILE), 0)
    lane = lax.broadcasted_iota(jnp.int32, (K, TILE), 1)
    places = jnp.zeros((K, TILE), F32)
    for t in range(SLOTS):
        live = jnp.full((K, TILE), t, jnp.int32) < jnp.full((K, TILE), count[0], jnp.int32)
        c = jnp.where(live, jnp.full((K, TILE), cols[t], jnp.int32), -1).astype(F32)
        r = jnp.where(live, jnp.full((K, TILE), rows[t], jnp.int32), -1).astype(F32)
        places = jnp.where((sub == i // 16) & (lane == lax.rem(i, 16) * SLOTS + t), c, places)
        places = jnp.where((sub == 2) & (lane == j * SLOTS + t), r, places)
    xcol[i * CHUNK + BLOCKS] = places
    xrow[j * CHUNK + BLOCKS] = places
    loads[0].wait()
    loads[1].wait()
    pl.semaphore_wait(barrier, len(near))

    def place(buf, t):
        slot = lax.rem(i - 2 * t + ROWS, ROWS)
        return buf.at[pl.ds(slot * CHUNK, CHUNK)] if buf is xcol else buf.at[slot]

    def onward(buf, n, rsem, hsem, t):
        at = place(buf, t)
        for u in (TREE if buf is xcol else LIST_TREE).get(t, ()):
            copy(at, at, sent.at[n], rsem.at[u + CHIPS // 2 - 1], chip(u - t)).start()
        copy(at, at, sent.at[n + 1], hsem.at[0], sib).start()

    def arrive(buf, n, rsem, hsem, hops):
        for t in hops:
            arrived(place(buf, t), rsem.at[t + CHIPS // 2 - 1])
            onward(buf, n, rsem, hsem, t)

    def over_plane(src, dst, n, rsem):
        for p in PLANE:
            copy(src, dst, sent.at[n], rsem.at[0], plane(p)).start()

    own = xrow.at[pl.ds(j * CHUNK, CHUNK)]
    onward(xcol, 0, xr, hr, 0)
    over_plane(own, own, 4, pr)

    for c in loads[2:5]:
        c.wait()
    for t in range(SLOTS):
        split_tile(tiles[t], parts.at[t])

    for t in range(SLOTS):
        split_tile(tiles[t].T, flipped.at[t])
    arrive(xcol, 0, xr, hr, WAVES[0])
    arrived(xrow.at[pl.ds(0, (COLS - 1) * CHUNK)], pr.at[0])

    for t in range(SLOTS):
        r = rows[t]
        v = xrow[r + lax.shift_right_logical(r, 4)]
        y = product(v, parts[t])
        for k in range(K):
            fsend[k, t : t + 1, :] = y[k : k + 1, :]
    fbuf[i] = fsend[...]
    onward(fbuf, 2, fr, gr, 0)

    arrive(xcol, 0, xr, hr, WAVES[1])
    arrive(fbuf, 2, fr, gr, LIST_WAVES[0])
    arrive(xcol, 0, xr, hr, WAVES[2])
    arrived(xcol.at[pl.ds(0, ROWS // 2 * CHUNK)], hr.at[0])

    for t in range(SLOTS):
        r = cols[t]
        v = xcol[r + lax.shift_right_logical(r, 4)]
        y = product(v, flipped[t])
        for k in range(K):
            dsend[k, t : t + 1, :] = y[k : k + 1, :]
    dbuf[j] = dsend[...]
    over_plane(dbuf.at[j], dbuf.at[j], 5, dr)
    arrive(fbuf, 2, fr, gr, LIST_WAVES[1])

    at_cols = jnp.zeros((K, TILE), F32)
    for d in range(ROWS):
        at_cols = at_cols + xcol[d * CHUNK + BLOCKS]
    at_rows = jnp.zeros((K, TILE), F32)
    for d in range(COLS):
        at_rows = at_rows + xrow[d * CHUNK + BLOCKS]
    block = lax.broadcasted_iota(jnp.int32, (BLOCKS, TILE), 0)

    def hot(line, first):
        return jnp.where(line.astype(jnp.int32) == block + first * BLOCKS, 1.0, 0.0).astype(F32)

    hot_low = hot(at_cols[0:1, :], i)
    hot_high = hot(at_cols[1:2, :], i)
    hot_row = hot(at_rows[2:3, :], j)

    x = [xcol[pl.ds(i * CHUNK, BLOCKS), k, :] for k in range(K)]
    old = [prev[:, k, :] for k in range(K)]
    res = []
    for k in range(K):
        r = energy[...] * x[k]
        for m in range(K):
            r = r - coupling[k, m] * old[m]
        res.append(r)

    gather[...] = jnp.zeros((TILE, TILE), F32)

    def inner(row, a, b):
        gather[row : row + 1, :] = jnp.sum(a * b, axis=0, keepdims=True)

    for k in range(K):
        for l in range(K):
            inner(4 * k + l, x[k], x[l])

    arrive(fbuf, 2, fr, gr, LIST_WAVES[2])
    arrived(fbuf.at[pl.ds(0, ROWS // 2)], gr.at[0])
    for k in range(K):
        low = fbuf[0:16, k].reshape(TILE, TILE)
        high = fbuf[16:32, k].reshape(TILE, TILE)
        res[k] = res[k] + (dot(hot_low, low) + dot(hot_high, high))
    arrived(dbuf.at[pl.ds(0, COLS - 1)], dr.at[0])
    for k in range(K):
        res[k] = res[k] + dot(hot_row, dbuf[:, k].reshape(TILE, TILE))

    for k in range(K):
        for l in range(K):
            inner(16 + 4 * k + l, x[k], res[l])
            inner(32 + 4 * k + l, res[k], res[l])
    here = dot(jnp.ones((8, TILE), F32), gather[...], trans_b=True)

    msg[0] = here[0:1]
    red1[j] = here[0:1]

    over_plane(msg.at[0], red1.at[j], 6, ar1)
    arrived(red1.at[pl.ds(0, COLS - 1)], ar1.at[0])
    part = sum_pairs(red1[...].reshape(COLS, TILE))
    msg[1] = part[0:1]
    red2[i] = part[0:1]

    for d in COLUMN:
        for other in (False, True):
            copy(msg.at[1], red2.at[i], sent.at[7], ar2.at[0], chip(d, other)).start()
    copy(msg.at[1], red2.at[i], sent.at[7], ar2.at[0], sib).start()
    arrived(red2.at[pl.ds(0, ROWS - 1)], ar2.at[0])

    sums = sum_pairs(red2[...].reshape(ROWS, TILE)) * (1.0 / TOTAL)

    g_km, g_km_low = pick(sums, 0, 1, 4, 0), pick(sums, 64, 1, 4, 0)
    f_ml = pick(sums, 16, 4, 0, 1)
    f_mk, f_mk_low = pick(sums, 16, 4, 1, 0), pick(sums, 80, 4, 1, 0)
    first = pltpu.roll(sums, TILE - 16, 1)
    gf, _ = fold_m(g_km * f_ml, jnp.zeros_like(g_km))
    alpha = first + (first - gf)
    a_ml, a_mk = pick(alpha, 0, 4, 0, 1), pick(alpha, 0, 4, 1, 0)
    p, e = two_prod(g_km, a_ml)
    p, e = fold_m(p, e + g_km_low * a_ml)
    p, r = two_sum(p, -first)
    e = e + r - pltpu.roll(sums, TILE - 80, 1)
    p, e = two_sum(p, e)
    t_ml, t_ml_low = pick(p, 0, 4, 0, 1), pick(e, 0, 4, 0, 1)
    p, e = two_prod(a_mk, t_ml)
    q, r = two_prod(-f_mk, a_ml)
    p, s = two_sum(p, q)
    p, e = fold_m(p, e + r + s + a_mk * t_ml_low - f_mk_low * a_ml)
    p, r = two_sum(p, pltpu.roll(sums, TILE - 32, 1))
    gram = p + (e + r + pltpu.roll(sums, TILE - 96, 1))

    def entry(v, k, l):
        return v[0:1, 4 * k + l : 4 * k + l + 1]

    low = {}
    inv = []
    for k in range(K):
        d = entry(gram, k, k)
        for m in range(k):
            d = d - low[k, m] * low[k, m]
        low[k, k] = jnp.sqrt(d)
        inv.append(1.0 / low[k, k])
        for n in range(k + 1, K):
            v = entry(gram, n, k)
            for m in range(k):
                v = v - low[n, m] * low[k, m]
            low[n, k] = v * inv[k]

    done = []
    for l in range(K):
        r = res[l]
        for k in range(K):
            r = r - entry(alpha, k, l) * x[k]
        for m in range(l):
            r = r - low[l, m] * done[m]
        done.append(r * inv[l])
    for k in range(K):
        next_ref[:, k, :] = done[k]

    row4 = lax.broadcasted_iota(jnp.int32, (K, K), 0)
    col4 = lax.broadcasted_iota(jnp.int32, (K, K), 1)
    a, b = jnp.zeros((K, K), F32), jnp.zeros((K, K), F32)
    for k in range(K):
        for l in range(K):
            a = jnp.where((row4 == k) & (col4 == l), entry(alpha, k, l), a)
            if l >= k:
                b = jnp.where((row4 == k) & (col4 == l), low[l, k], b)
    alpha_ref[...] = a
    beta_ref[...] = b

    left(xcol.at[pl.ds(0, (CHIPS - 1) * CHUNK)], sent.at[0])
    left(xcol.at[pl.ds(0, CHIPS * CHUNK)], sent.at[1])
    left(fbuf.at[pl.ds(0, CHIPS - 1)], sent.at[2])
    left(fbuf.at[pl.ds(0, CHIPS)], sent.at[3])
    left(xrow.at[pl.ds(0, (COLS - 1) * CHUNK)], sent.at[4])
    left(dbuf.at[pl.ds(0, COLS - 1)], sent.at[5])
    left(red1.at[pl.ds(0, COLS - 1)], sent.at[6])
    left(red2.at[pl.ds(0, ROWS - 1)], sent.at[7])


def hand_over(*refs):
    n = len(refs) // 2
    sems = refs[-1]
    copies = [pltpu.make_async_copy(refs[k], refs[n + k], sems.at[k]) for k in range(n)]
    for c in copies:
        c.start()
    for c in copies:
        c.wait()


def step(tiles, tile_rows, tile_cols, tile_count, energy, basis_block, previous_block, coupling):
    vmem, hbm = (pl.BlockSpec(memory_space=m) for m in (pltpu.VMEM, pl.ANY))
    dma = pltpu.SemaphoreType.DMA
    def blocked(a):
        return a.reshape(K, BLOCKS, TILE).transpose(1, 0, 2)

    operands = (
        tile_rows, tile_cols, coupling, tiles, energy.reshape(BLOCKS, TILE),
        blocked(basis_block), blocked(previous_block),
    )
    out, alpha, beta = pl.pallas_call(
        body,
        out_shape=(
            pltpu.VMEM((BLOCKS, K, TILE), F32),
            pltpu.VMEM((K, K), F32),
            pltpu.VMEM((K, K), F32),
        ),
        in_specs=[pl.BlockSpec(memory_space=pltpu.SMEM)] + [hbm] * 7,
        out_specs=(vmem, vmem, vmem),
        scratch_shapes=[
            pltpu.SMEM((SLOTS,), jnp.int32),
            pltpu.SMEM((SLOTS,), jnp.int32),
            pltpu.SMEM((K, K), F32),
            pltpu.VMEM((ROWS * CHUNK, K, TILE), F32),
            pltpu.VMEM((COLS * CHUNK, K, TILE), F32),
            pltpu.VMEM((SLOTS, TILE, TILE), F32),
            pltpu.VMEM((SLOTS, 3 * TILE, TILE), jnp.bfloat16),
            pltpu.VMEM((SLOTS, 3 * TILE, TILE), jnp.bfloat16),
            pltpu.VMEM((BLOCKS, TILE), F32),
            pltpu.VMEM((BLOCKS, K, TILE), F32),
            pltpu.VMEM((K, SLOTS, TILE), F32),
            pltpu.VMEM((ROWS, K, SLOTS, TILE), F32),
            pltpu.VMEM((K, SLOTS, TILE), F32),
            pltpu.VMEM((COLS, K, SLOTS, TILE), F32),
            pltpu.VMEM((TILE, TILE), F32),
            pltpu.VMEM((COLS, 1, TILE), F32),
            pltpu.VMEM((ROWS, 1, TILE), F32),
            pltpu.VMEM((2, 1, TILE), F32),
            dma((8,)),
            dma((8,)),
            dma((CHIPS,)), dma((1,)), dma((1,)),
            dma((CHIPS,)), dma((1,)), dma((1,)),
            dma((1,)), dma((1,)),
        ],
        compiler_params=pltpu.CompilerParams(
            collective_id=0, has_side_effects=True, vmem_limit_bytes=32 << 20
        ),
        name="lanczos",
    )(tile_count, *(pltpu.with_memory_space_constraint(a, pltpu.HBM) for a in operands))
    results = (out, alpha, beta)
    out, alpha, beta = pl.pallas_call(
        hand_over,
        out_shape=tuple(jax.ShapeDtypeStruct(r.shape, F32) for r in results),
        in_specs=[hbm] * 3,
        out_specs=(hbm,) * 3,
        scratch_shapes=[dma((3,))],
        compiler_params=pltpu.CompilerParams(vmem_limit_bytes=1 << 20),
        name="hand_over",
    )(*results)
    return out.transpose(1, 0, 2).reshape(K, WIDTH), alpha, beta


def solution(mesh):
    both = ("row", "col")
    return jax.shard_map(
        step,
        mesh=mesh,
        in_specs=(
            P(both, None, None), P(both), P(both), P(both), P(both), P(None, both), P(None, both), P(),
        ),
        out_specs=(P(None, both), P(), P()),
        check_vma=False,
    )
```

```python
import jax
import jax.numpy as jnp
from jax import lax
from jax.experimental import pallas as pl
from jax.experimental.pallas import tpu as pltpu
from jax.sharding import PartitionSpec as P

MESH = pl.DeviceIdType.MESH
HIGH = lax.Precision.HIGHEST
F32 = jnp.float32
ROWS, COLS, CHIPS = 32, 16, 16
K, SLOTS, TILE, WIDTH = 4, 8, 128, 2048
BLOCKS = WIDTH // TILE
CHUNK = BLOCKS + 1
TOTAL = float(WIDTH * ROWS * COLS)
TREE = {
    0: (3, -3, 1, -1),
    3: (6, 4, 2), -3: (-6, -4, -2),
    6: (8, 7, 5), -6: (-7, -5),
}
WAVES = (1, -1, 3, -3), (2, -2, 4, -4, 6, -6), (5, -5, 7, -7, 8)
LIST_TREE = {0: (3, -3, 1, -1), 3: (6, 4, 2), -3: (-6, -4, -2), 6: (8, 7, 5), -6: (-7, -5)}
LIST_WAVES = ((1, -1, 3, -3), (2, -2, 4, -4, 6, -6), (5, -5, 7, -7, 8))
RING = {0: 0, 1: 1, 2: 2, 3: 1}
PLANE = sorted(
    ((dx, dy) for dx in range(4) for dy in range(4) if dx or dy), key=lambda p: -RING[p[0]] - RING[p[1]]
)
COLUMN = sorted(range(1, CHIPS), key=lambda d: -min(d, CHIPS - d))


def dot(a, b, trans_b=False):
    dims = (((1,), (1 if trans_b else 0,)), ((), ()))
    return lax.dot_general(a, b, dims, precision=HIGH, preferred_element_type=F32)


def thirds(a):
    parts = []
    for _ in range(3):
        p = a.astype(jnp.bfloat16).astype(F32)
        parts.append(p)
        a = a - p
    return parts


def split_tile(tile, out):
    for n, p in enumerate(thirds(tile)):
        out[n * TILE : (n + 1) * TILE, :] = p.astype(jnp.bfloat16)


def product(x, tile):
    left = jnp.concatenate(thirds(x) + [jnp.zeros_like(x)], axis=0).astype(jnp.bfloat16)
    y = lax.dot_general(
        jnp.concatenate([left] * 3, axis=1), tile, (((1,), (0,)), ((), ())), preferred_element_type=F32
    )
    return (y[8:12] + y[4:8]) + y[0:4]


def two_sum(a, b):
    s = a + b
    t = s - a
    return s, (a - (s - t)) + (b - t)


def split(a):
    c = a * 4097.0
    high = c - (c - a)
    return high, a - high


def two_prod(a, b):
    p = a * b
    ah, al = split(a)
    bh, bl = split(b)
    return p, ((ah * bh - p) + ah * bl + al * bh) + al * bl


def fold_rows(x, e):
    for s in (4, 2, 1):
        x, r = two_sum(x, pltpu.roll(x, s, 0))
        e = e + pltpu.roll(e, s, 0) + r
    return x, e


def sum_pairs(rows):
    x, e = rows[0:8], jnp.zeros((8, TILE), F32)
    for r in range(8, rows.shape[0], 8):
        x, t = two_sum(x, rows[r : r + 8])
        e = e + t
    x, e = fold_rows(x, e)
    lane = lax.broadcasted_iota(jnp.int32, (8, TILE), 1)
    return x + jnp.where(lane >= 64, pltpu.roll(e, 64, 1), 0.0)


def pick(row, base, stride_m, stride_k, stride_l):
    lane = lax.broadcasted_iota(jnp.int32, (8, TILE), 1)
    src = base + stride_k * (lane // 4 % 4) + stride_l * (lane % 4)
    return [jnp.take_along_axis(row, src + stride_m * m, axis=1, mode="promise_in_bounds") for m in range(K)]


def entry(row, k, l):
    src = jnp.full((8, TILE), 4 * k + l, jnp.int32)
    return jnp.take_along_axis(row, src, axis=1, mode="promise_in_bounds")


def times(v, plane):
    return (plane.reshape(2, 8, TILE) * v).reshape(BLOCKS, TILE)


def body(count, rows_hbm, cols_hbm, coupling_hbm, tiles_hbm, energy_hbm, basis_hbm, prev_hbm,
         next_ref, alpha_ref, beta_ref,
         rows, cols, coupling, xcol, xrow, tiles, parts, flipped, energy, prev, fsend, fbuf, dsend, dbuf, gather, red1, red2, msg,
         local, sent, xr, hr, pr, fr, gr, dr, ar1, ar2):
    i, j = lax.axis_index("row"), lax.axis_index("col")
    sib = (i + 1 - 2 * lax.rem(i, 2), j)

    def chip(d, other=False):
        core = lax.rem(i, 2)
        return (2 * lax.rem(i // 2 + d + CHIPS, CHIPS) + (1 - core if other else core), j)

    def plane(p):
        return (i, 4 * lax.rem(j // 4 + p[0], 4) + lax.rem(lax.rem(j, 4) + p[1], 4))

    def copy(src, dst, s, r, dev):
        return pltpu.make_async_remote_copy(
            src_ref=src, dst_ref=dst, send_sem=s, recv_sem=r, device_id=dev, device_id_type=MESH
        )

    def arrived(ref, sem):
        copy(ref, ref, sem, sem, sib).wait_recv()

    def left(ref, sem):
        copy(ref, ref, sem, sem, sib).wait_send()

    loads = [
        pltpu.make_async_copy(basis_hbm, xcol.at[pl.ds(i * CHUNK, BLOCKS)], local.at[0]),
        pltpu.make_async_copy(basis_hbm, xrow.at[pl.ds(j * CHUNK, BLOCKS)], local.at[1]),
        pltpu.make_async_copy(tiles_hbm, tiles, local.at[2]),
        pltpu.make_async_copy(energy_hbm, energy, local.at[3]),
        pltpu.make_async_copy(prev_hbm, prev, local.at[4]),
        pltpu.make_async_copy(rows_hbm, rows, local.at[5]),
        pltpu.make_async_copy(cols_hbm, cols, local.at[6]),
        pltpu.make_async_copy(coupling_hbm, coupling, local.at[7]),
    ]
    for c in loads:
        c.start()

    barrier = pltpu.get_barrier_semaphore()
    near = [chip(s * d) for d in (3, 2, 1) for s in (1, -1)] + [plane(p) for p in PLANE] + [sib]
    for dev in near:
        pl.semaphore_signal(barrier, inc=1, device_id=dev, device_id_type=MESH)

    for c in loads[5:]:
        c.wait()

    sub = lax.broadcasted_iota(jnp.int32, (K, TILE), 0)
    lane = lax.broadcasted_iota(jnp.int32, (K, TILE), 1)
    places = jnp.zeros((K, TILE), F32)
    for t in range(SLOTS):
        live = jnp.full((K, TILE), t, jnp.int32) < jnp.full((K, TILE), count[0], jnp.int32)
        c = jnp.where(live, jnp.full((K, TILE), cols[t], jnp.int32), -1).astype(F32)
        r = jnp.where(live, jnp.full((K, TILE), rows[t], jnp.int32), -1).astype(F32)
        places = jnp.where((sub == i // 16) & (lane == lax.rem(i, 16) * SLOTS + t), c, places)
        places = jnp.where((sub == 2) & (lane == j * SLOTS + t), r, places)
    xcol[i * CHUNK + BLOCKS] = places
    xrow[j * CHUNK + BLOCKS] = places
    loads[0].wait()
    loads[1].wait()
    pl.semaphore_wait(barrier, len(near))

    def place(buf, t):
        slot = lax.rem(i - 2 * t + ROWS, ROWS)
        return buf.at[pl.ds(slot * CHUNK, CHUNK)] if buf is xcol else buf.at[slot]

    def onward(buf, n, rsem, hsem, t):
        at = place(buf, t)
        for u in (TREE if buf is xcol else LIST_TREE).get(t, ()):
            copy(at, at, sent.at[n], rsem.at[u + CHIPS // 2 - 1], chip(u - t)).start()
        copy(at, at, sent.at[n + 1], hsem.at[0], sib).start()

    def arrive(buf, n, rsem, hsem, hops):
        for t in hops:
            arrived(place(buf, t), rsem.at[t + CHIPS // 2 - 1])
            onward(buf, n, rsem, hsem, t)

    def over_plane(src, dst, n, rsem):
        for p in PLANE:
            copy(src, dst, sent.at[n], rsem.at[0], plane(p)).start()

    own = xrow.at[pl.ds(j * CHUNK, CHUNK)]
    onward(xcol, 0, xr, hr, 0)
    over_plane(own, own, 4, pr)

    for c in loads[2:5]:
        c.wait()
    for t in range(SLOTS):
        split_tile(tiles[t], parts.at[t])

    for t in range(SLOTS):
        split_tile(tiles[t].T, flipped.at[t])
    arrive(xcol, 0, xr, hr, WAVES[0])
    arrived(xrow.at[pl.ds(0, (COLS - 1) * CHUNK)], pr.at[0])

    for t in range(SLOTS):
        r = rows[t]
        v = xrow[r + lax.shift_right_logical(r, 4)]
        y = product(v, parts[t])
        for k in range(K):
            fsend[k, t : t + 1, :] = y[k : k + 1, :]
    fbuf[i] = fsend[...]
    onward(fbuf, 2, fr, gr, 0)

    arrive(xcol, 0, xr, hr, WAVES[1])
    arrive(fbuf, 2, fr, gr, LIST_WAVES[0])
    arrive(xcol, 0, xr, hr, WAVES[2])
    arrived(xcol.at[pl.ds(0, ROWS // 2 * CHUNK)], hr.at[0])

    for t in range(SLOTS):
        r = cols[t]
        v = xcol[r + lax.shift_right_logical(r, 4)]
        y = product(v, flipped[t])
        for k in range(K):
            dsend[k, t : t + 1, :] = y[k : k + 1, :]
    dbuf[j] = dsend[...]
    over_plane(dbuf.at[j], dbuf.at[j], 5, dr)
    arrive(fbuf, 2, fr, gr, LIST_WAVES[1])

    at_cols = jnp.zeros((K, TILE), F32)
    for d in range(ROWS):
        at_cols = at_cols + xcol[d * CHUNK + BLOCKS]
    at_rows = jnp.zeros((K, TILE), F32)
    for d in range(COLS):
        at_rows = at_rows + xrow[d * CHUNK + BLOCKS]
    block = lax.broadcasted_iota(jnp.int32, (BLOCKS, TILE), 0)

    def hot(line, first):
        return jnp.where(line.astype(jnp.int32) == block + first * BLOCKS, 1.0, 0.0).astype(F32)

    hot_low = hot(at_cols[0:1, :], i)
    hot_high = hot(at_cols[1:2, :], i)
    hot_row = hot(at_rows[2:3, :], j)

    x = [xcol[pl.ds(i * CHUNK, BLOCKS), k, :] for k in range(K)]
    old = [prev[:, k, :] for k in range(K)]
    res = []
    for k in range(K):
        r = energy[...] * x[k]
        for m in range(K):
            r = r - coupling[k, m] * old[m]
        res.append(r)

    gather[...] = jnp.zeros((TILE, TILE), F32)

    def inner(row, a, b):
        gather[row : row + 1, :] = jnp.sum(a * b, axis=0, keepdims=True)

    for k in range(K):
        for l in range(K):
            inner(4 * k + l, x[k], x[l])

    arrive(fbuf, 2, fr, gr, LIST_WAVES[2])
    arrived(fbuf.at[pl.ds(0, ROWS // 2)], gr.at[0])
    for k in range(K):
        low = fbuf[0:16, k].reshape(TILE, TILE)
        high = fbuf[16:32, k].reshape(TILE, TILE)
        res[k] = res[k] + (dot(hot_low, low) + dot(hot_high, high))
    arrived(dbuf.at[pl.ds(0, COLS - 1)], dr.at[0])
    for k in range(K):
        res[k] = res[k] + dot(hot_row, dbuf[:, k].reshape(TILE, TILE))

    for k in range(K):
        for l in range(K):
            inner(16 + 4 * k + l, x[k], res[l])
            inner(32 + 4 * k + l, res[k], res[l])
    here = dot(jnp.ones((8, TILE), F32), gather[...], trans_b=True)

    msg[0] = here[0:1]
    red1[j] = here[0:1]

    over_plane(msg.at[0], red1.at[j], 6, ar1)
    arrived(red1.at[pl.ds(0, COLS - 1)], ar1.at[0])
    part = sum_pairs(red1[...].reshape(COLS, TILE))
    msg[1] = part[0:1]
    red2[i] = part[0:1]

    for d in COLUMN:
        for other in (False, True):
            copy(msg.at[1], red2.at[i], sent.at[7], ar2.at[0], chip(d, other)).start()
    copy(msg.at[1], red2.at[i], sent.at[7], ar2.at[0], sib).start()
    arrived(red2.at[pl.ds(0, ROWS - 1)], ar2.at[0])

    sums = sum_pairs(red2[...].reshape(ROWS, TILE)) * (1.0 / TOTAL)

    g_km, g_km_low = pick(sums, 0, 1, 4, 0), pick(sums, 64, 1, 4, 0)
    f_ml = pick(sums, 16, 4, 0, 1)
    f_mk, f_mk_low = pick(sums, 16, 4, 1, 0), pick(sums, 80, 4, 1, 0)
    first, first_low = pltpu.roll(sums, TILE - 16, 1), pltpu.roll(sums, TILE - 80, 1)
    resid, resid_low = pltpu.roll(sums, TILE - 32, 1), pltpu.roll(sums, TILE - 96, 1)
    gf = (g_km[0] * f_ml[0] + g_km[1] * f_ml[1]) + (g_km[2] * f_ml[2] + g_km[3] * f_ml[3])
    alpha = first + (first - gf)
    a_ml, a_mk = pick(alpha, 0, 4, 0, 1), pick(alpha, 0, 4, 1, 0)
    p, e = -first, -first_low
    for m in range(K):
        q, r = two_prod(g_km[m], a_ml[m])
        p, t = two_sum(p, q)
        e = e + (r + t + g_km_low[m] * a_ml[m])
    p, e = two_sum(p, e)
    t_ml, t_ml_low = pick(p, 0, 4, 0, 1), pick(e, 0, 4, 0, 1)
    p, e = resid, resid_low
    for m in range(K):
        q, r = two_prod(-f_mk[m], a_ml[m])
        p, t = two_sum(p, q)
        e = e + (r + t - f_mk_low[m] * a_ml[m])
    for m in range(K):
        q, r = two_prod(a_mk[m], t_ml[m])
        p, t = two_sum(p, q)
        e = e + (r + t + a_mk[m] * t_ml_low[m])
    gram = p + e

    low = {}
    inv = []
    for k in range(K):
        d = entry(gram, k, k)
        for m in range(k):
            d = d - low[k, m] * low[k, m]
        inv.append(lax.rsqrt(d))
        low[k, k] = d * inv[k]
        for n in range(k + 1, K):
            v = entry(gram, n, k)
            for m in range(k):
                v = v - low[n, m] * low[k, m]
            low[n, k] = v * inv[k]

    done = []
    for l in range(K):
        r = res[l]
        for k in range(K):
            r = r - times(entry(alpha, k, l), x[k])
        for m in range(l):
            r = r - times(low[l, m], done[m])
        done.append(times(inv[l], r))
    for k in range(K):
        next_ref[:, k, :] = done[k]

    sub = lax.broadcasted_iota(jnp.int32, (8, TILE), 0)
    lane = lax.broadcasted_iota(jnp.int32, (8, TILE), 1)
    a, b = jnp.zeros((8, TILE), F32), jnp.zeros((8, TILE), F32)
    for k in range(K):
        for l in range(K):
            a = jnp.where((sub == k) & (lane == l), entry(alpha, k, l), a)
            if l >= k:
                b = jnp.where((sub == k) & (lane == l), low[l, k], b)
    alpha_ref[...] = a[0:K, 0:K]
    beta_ref[...] = b[0:K, 0:K]

    left(xcol.at[pl.ds(0, (CHIPS - 1) * CHUNK)], sent.at[0])
    left(xcol.at[pl.ds(0, CHIPS * CHUNK)], sent.at[1])
    left(fbuf.at[pl.ds(0, CHIPS - 1)], sent.at[2])
    left(fbuf.at[pl.ds(0, CHIPS)], sent.at[3])
    left(xrow.at[pl.ds(0, (COLS - 1) * CHUNK)], sent.at[4])
    left(dbuf.at[pl.ds(0, COLS - 1)], sent.at[5])
    left(red1.at[pl.ds(0, COLS - 1)], sent.at[6])
    left(red2.at[pl.ds(0, ROWS - 1)], sent.at[7])


def hand_over(*refs):
    n = len(refs) // 2
    sems = refs[-1]
    copies = [pltpu.make_async_copy(refs[k], refs[n + k], sems.at[k]) for k in range(n)]
    for c in copies:
        c.start()
    for c in copies:
        c.wait()


def step(tiles, tile_rows, tile_cols, tile_count, energy, basis_block, previous_block, coupling):
    vmem, hbm = (pl.BlockSpec(memory_space=m) for m in (pltpu.VMEM, pl.ANY))
    dma = pltpu.SemaphoreType.DMA
    def blocked(a):
        return a.reshape(K, BLOCKS, TILE).transpose(1, 0, 2)

    operands = (
        tile_rows, tile_cols, coupling, tiles, energy.reshape(BLOCKS, TILE),
        blocked(basis_block), blocked(previous_block),
    )
    out, alpha, beta = pl.pallas_call(
        body,
        out_shape=(
            pltpu.VMEM((BLOCKS, K, TILE), F32),
            pltpu.VMEM((K, K), F32),
            pltpu.VMEM((K, K), F32),
        ),
        in_specs=[pl.BlockSpec(memory_space=pltpu.SMEM)] + [hbm] * 7,
        out_specs=(vmem, vmem, vmem),
        scratch_shapes=[
            pltpu.SMEM((SLOTS,), jnp.int32),
            pltpu.SMEM((SLOTS,), jnp.int32),
            pltpu.SMEM((K, K), F32),
            pltpu.VMEM((ROWS * CHUNK, K, TILE), F32),
            pltpu.VMEM((COLS * CHUNK, K, TILE), F32),
            pltpu.VMEM((SLOTS, TILE, TILE), F32),
            pltpu.VMEM((SLOTS, 3 * TILE, TILE), jnp.bfloat16),
            pltpu.VMEM((SLOTS, 3 * TILE, TILE), jnp.bfloat16),
            pltpu.VMEM((BLOCKS, TILE), F32),
            pltpu.VMEM((BLOCKS, K, TILE), F32),
            pltpu.VMEM((K, SLOTS, TILE), F32),
            pltpu.VMEM((ROWS, K, SLOTS, TILE), F32),
            pltpu.VMEM((K, SLOTS, TILE), F32),
            pltpu.VMEM((COLS, K, SLOTS, TILE), F32),
            pltpu.VMEM((TILE, TILE), F32),
            pltpu.VMEM((COLS, 1, TILE), F32),
            pltpu.VMEM((ROWS, 1, TILE), F32),
            pltpu.VMEM((2, 1, TILE), F32),
            dma((8,)),
            dma((8,)),
            dma((CHIPS,)), dma((1,)), dma((1,)),
            dma((CHIPS,)), dma((1,)), dma((1,)),
            dma((1,)), dma((1,)),
        ],
        compiler_params=pltpu.CompilerParams(
            collective_id=0, has_side_effects=True, vmem_limit_bytes=32 << 20
        ),
        name="lanczos",
    )(tile_count, *(pltpu.with_memory_space_constraint(a, pltpu.HBM) for a in operands))
    results = (out, alpha, beta)
    out, alpha, beta = pl.pallas_call(
        hand_over,
        out_shape=tuple(jax.ShapeDtypeStruct(r.shape, F32) for r in results),
        in_specs=[hbm] * 3,
        out_specs=(hbm,) * 3,
        scratch_shapes=[dma((3,))],
        compiler_params=pltpu.CompilerParams(vmem_limit_bytes=1 << 20),
        name="hand_over",
    )(*results)
    return out.transpose(1, 0, 2).reshape(K, WIDTH), alpha, beta


def solution(mesh):
    both = ("row", "col")
    return jax.shard_map(
        step,
        mesh=mesh,
        in_specs=(
            P(both, None, None), P(both), P(both), P(both), P(both), P(None, both), P(None, both), P(),
        ),
        out_specs=(P(None, both), P(), P()),
        check_vma=False,
    )
```

```python
import jax
import jax.numpy as jnp
from jax import lax
from jax.experimental import pallas as pl
from jax.experimental.pallas import tpu as pltpu
from jax.sharding import PartitionSpec as P

MESH = pl.DeviceIdType.MESH
HIGH = lax.Precision.HIGHEST
F32 = jnp.float32
ROWS, COLS, CHIPS = 32, 16, 16
K, SLOTS, TILE, WIDTH = 4, 8, 128, 2048
BLOCKS = WIDTH // TILE
CHUNK = BLOCKS + 1
TOTAL = float(WIDTH * ROWS * COLS)
TREE = {
    0: (3, -3, 1, -1),
    3: (6, 4, 2), -3: (-6, -4, -2),
    6: (8, 7, 5), -6: (-7, -5),
}
WAVES = (3, -3, 1, -1), (6, -6, 2, -2, 4, -4), (5, -5, 7, -7, 8)
LIST_TREE = {0: (3, -3, 1, -1), 3: (6, 4, 2), -3: (-6, -4, -2), 6: (8, 7, 5), -6: (-7, -5)}
LIST_WAVES = ((3, -3, 1, -1), (6, -6, 2, -2, 4, -4), (5, -5, 7, -7, 8))
RING = {0: 0, 1: 1, 2: 2, 3: 1}
PLANE = sorted(
    ((dx, dy) for dx in range(4) for dy in range(4) if dx or dy), key=lambda p: -RING[p[0]] - RING[p[1]]
)
COLUMN = sorted(range(1, CHIPS), key=lambda d: -min(d, CHIPS - d))


def dot(a, b, trans_b=False):
    dims = (((1,), (1 if trans_b else 0,)), ((), ()))
    return lax.dot_general(a, b, dims, precision=HIGH, preferred_element_type=F32)


def thirds(a):
    parts = []
    for _ in range(3):
        p = a.astype(jnp.bfloat16).astype(F32)
        parts.append(p)
        a = a - p
    return parts


def split_tile(tile, out):
    for n, p in enumerate(thirds(tile)):
        out[n * TILE : (n + 1) * TILE, :] = p.astype(jnp.bfloat16)


def product(x, tile):
    left = jnp.concatenate(thirds(x) + [jnp.zeros_like(x)], axis=0).astype(jnp.bfloat16)
    y = lax.dot_general(
        jnp.concatenate([left] * 3, axis=1), tile, (((1,), (0,)), ((), ())), preferred_element_type=F32
    )
    return (y[8:12] + y[4:8]) + y[0:4]


def two_sum(a, b):
    s = a + b
    t = s - a
    return s, (a - (s - t)) + (b - t)


def split(a):
    c = a * 4097.0
    high = c - (c - a)
    return high, a - high


def two_prod(a, b):
    p = a * b
    ah, al = split(a)
    bh, bl = split(b)
    return p, ((ah * bh - p) + ah * bl + al * bh) + al * bl


def fold_rows(x, e):
    for s in (4, 2, 1):
        x, r = two_sum(x, pltpu.roll(x, s, 0))
        e = e + pltpu.roll(e, s, 0) + r
    return x, e


def sum_pairs(rows):
    x, e = rows[0:8], jnp.zeros((8, TILE), F32)
    for r in range(8, rows.shape[0], 8):
        x, t = two_sum(x, rows[r : r + 8])
        e = e + t
    x, e = fold_rows(x, e)
    lane = lax.broadcasted_iota(jnp.int32, (8, TILE), 1)
    return x + jnp.where(lane >= 64, pltpu.roll(e, 64, 1), 0.0)


def pick(row, base, stride_m, stride_k, stride_l):
    lane = lax.broadcasted_iota(jnp.int32, (8, TILE), 1)
    src = base + stride_k * (lane // 4 % 4) + stride_l * (lane % 4)
    return [jnp.take_along_axis(row, src + stride_m * m, axis=1, mode="promise_in_bounds") for m in range(K)]


def entry(row, k, l):
    src = jnp.full((8, TILE), 4 * k + l, jnp.int32)
    return jnp.take_along_axis(row, src, axis=1, mode="promise_in_bounds")


def times(v, plane):
    return (plane.reshape(2, 8, TILE) * v).reshape(BLOCKS, TILE)


def body(count, rows_hbm, cols_hbm, coupling_hbm, tiles_hbm, energy_hbm, basis_hbm, prev_hbm,
         next_ref, alpha_ref, beta_ref,
         rows, cols, coupling, xcol, xrow, tiles, parts, flipped, energy, prev, fsend, fbuf, dsend, dbuf, gather, red1, red2, msg,
         local, sent, xr, hr, pr, fr, gr, dr, ar1, ar2):
    i, j = lax.axis_index("row"), lax.axis_index("col")
    sib = (i + 1 - 2 * lax.rem(i, 2), j)

    def chip(d, other=False):
        core = lax.rem(i, 2)
        return (2 * lax.rem(i // 2 + d + CHIPS, CHIPS) + (1 - core if other else core), j)

    def plane(p):
        return (i, 4 * lax.rem(j // 4 + p[0], 4) + lax.rem(lax.rem(j, 4) + p[1], 4))

    def copy(src, dst, s, r, dev):
        return pltpu.make_async_remote_copy(
            src_ref=src, dst_ref=dst, send_sem=s, recv_sem=r, device_id=dev, device_id_type=MESH
        )

    def arrived(ref, sem):
        copy(ref, ref, sem, sem, sib).wait_recv()

    def left(ref, sem):
        copy(ref, ref, sem, sem, sib).wait_send()

    loads = [
        pltpu.make_async_copy(basis_hbm, xcol.at[pl.ds(i * CHUNK, BLOCKS)], local.at[0]),
        pltpu.make_async_copy(basis_hbm, xrow.at[pl.ds(j * CHUNK, BLOCKS)], local.at[1]),
        pltpu.make_async_copy(tiles_hbm, tiles, local.at[2]),
        pltpu.make_async_copy(energy_hbm, energy, local.at[3]),
        pltpu.make_async_copy(prev_hbm, prev, local.at[4]),
        pltpu.make_async_copy(rows_hbm, rows, local.at[5]),
        pltpu.make_async_copy(cols_hbm, cols, local.at[6]),
        pltpu.make_async_copy(coupling_hbm, coupling, local.at[7]),
    ]
    for c in loads:
        c.start()

    barrier = pltpu.get_barrier_semaphore()
    near = [chip(s * d) for d in (3, 2, 1) for s in (1, -1)] + [plane(p) for p in PLANE] + [sib]
    for dev in near:
        pl.semaphore_signal(barrier, inc=1, device_id=dev, device_id_type=MESH)

    for c in loads[5:]:
        c.wait()

    sub = lax.broadcasted_iota(jnp.int32, (K, TILE), 0)
    lane = lax.broadcasted_iota(jnp.int32, (K, TILE), 1)
    places = jnp.zeros((K, TILE), F32)
    for t in range(SLOTS):
        live = jnp.full((K, TILE), t, jnp.int32) < jnp.full((K, TILE), count[0], jnp.int32)
        c = jnp.where(live, jnp.full((K, TILE), cols[t], jnp.int32), -1).astype(F32)
        r = jnp.where(live, jnp.full((K, TILE), rows[t], jnp.int32), -1).astype(F32)
        places = jnp.where((sub == i // 16) & (lane == lax.rem(i, 16) * SLOTS + t), c, places)
        places = jnp.where((sub == 2) & (lane == j * SLOTS + t), r, places)
    xcol[i * CHUNK + BLOCKS] = places
    xrow[j * CHUNK + BLOCKS] = places
    loads[0].wait()
    loads[1].wait()
    pl.semaphore_wait(barrier, len(near))

    def place(buf, t):
        slot = lax.rem(i - 2 * t + ROWS, ROWS)
        return buf.at[pl.ds(slot * CHUNK, CHUNK)] if buf is xcol else buf.at[slot]

    def onward(buf, n, rsem, hsem, t):
        at = place(buf, t)
        for u in (TREE if buf is xcol else LIST_TREE).get(t, ()):
            copy(at, at, sent.at[n], rsem.at[u + CHIPS // 2 - 1], chip(u - t)).start()
        copy(at, at, sent.at[n + 1], hsem.at[0], sib).start()

    def arrive(buf, n, rsem, hsem, hops):
        for t in hops:
            arrived(place(buf, t), rsem.at[t + CHIPS // 2 - 1])
            onward(buf, n, rsem, hsem, t)

    def over_plane(src, dst, n, rsem):
        for p in PLANE:
            copy(src, dst, sent.at[n], rsem.at[0], plane(p)).start()

    own = xrow.at[pl.ds(j * CHUNK, CHUNK)]
    onward(xcol, 0, xr, hr, 0)
    over_plane(own, own, 4, pr)

    for c in loads[2:5]:
        c.wait()
    for t in range(SLOTS):
        split_tile(tiles[t], parts.at[t])

    for t in range(SLOTS):
        split_tile(tiles[t].T, flipped.at[t])
    arrive(xcol, 0, xr, hr, WAVES[0])
    arrived(xrow.at[pl.ds(0, (COLS - 1) * CHUNK)], pr.at[0])

    for t in range(SLOTS):
        r = rows[t]
        v = xrow[r + lax.shift_right_logical(r, 4)]
        y = product(v, parts[t])
        for k in range(K):
            fsend[k, t : t + 1, :] = y[k : k + 1, :]
    fbuf[i] = fsend[...]
    onward(fbuf, 2, fr, gr, 0)

    arrive(xcol, 0, xr, hr, WAVES[1])
    arrive(fbuf, 2, fr, gr, LIST_WAVES[0])
    arrive(xcol, 0, xr, hr, WAVES[2])
    arrived(xcol.at[pl.ds(0, ROWS // 2 * CHUNK)], hr.at[0])

    for t in range(SLOTS):
        r = cols[t]
        v = xcol[r + lax.shift_right_logical(r, 4)]
        y = product(v, flipped[t])
        for k in range(K):
            dsend[k, t : t + 1, :] = y[k : k + 1, :]
    dbuf[j] = dsend[...]
    over_plane(dbuf.at[j], dbuf.at[j], 5, dr)
    arrive(fbuf, 2, fr, gr, LIST_WAVES[1])

    at_cols = jnp.zeros((K, TILE), F32)
    for d in range(ROWS):
        at_cols = at_cols + xcol[d * CHUNK + BLOCKS]
    at_rows = jnp.zeros((K, TILE), F32)
    for d in range(COLS):
        at_rows = at_rows + xrow[d * CHUNK + BLOCKS]
    block = lax.broadcasted_iota(jnp.int32, (BLOCKS, TILE), 0)

    def hot(line, first):
        return jnp.where(line.astype(jnp.int32) == block + first * BLOCKS, 1.0, 0.0).astype(F32)

    hot_low = hot(at_cols[0:1, :], i)
    hot_high = hot(at_cols[1:2, :], i)
    hot_row = hot(at_rows[2:3, :], j)

    x = [xcol[pl.ds(i * CHUNK, BLOCKS), k, :] for k in range(K)]
    old = [prev[:, k, :] for k in range(K)]
    res = []
    for k in range(K):
        r = energy[...] * x[k]
        for m in range(K):
            r = r - coupling[k, m] * old[m]
        res.append(r)

    gather[...] = jnp.zeros((TILE, TILE), F32)

    def inner(row, a, b):
        gather[row : row + 1, :] = jnp.sum(a * b, axis=0, keepdims=True)

    for k in range(K):
        for l in range(K):
            inner(4 * k + l, x[k], x[l])

    arrive(fbuf, 2, fr, gr, LIST_WAVES[2])
    arrived(fbuf.at[pl.ds(0, ROWS // 2)], gr.at[0])
    for k in range(K):
        low = fbuf[0:16, k].reshape(TILE, TILE)
        high = fbuf[16:32, k].reshape(TILE, TILE)
        res[k] = res[k] + (dot(hot_low, low) + dot(hot_high, high))
    arrived(dbuf.at[pl.ds(0, COLS - 1)], dr.at[0])
    for k in range(K):
        res[k] = res[k] + dot(hot_row, dbuf[:, k].reshape(TILE, TILE))

    for k in range(K):
        for l in range(K):
            inner(16 + 4 * k + l, x[k], res[l])
            if k <= l:
                both = jnp.sum(res[k] * res[l], axis=0, keepdims=True)
                gather[32 + 4 * k + l : 33 + 4 * k + l, :] = both
                gather[32 + 4 * l + k : 33 + 4 * l + k, :] = both
    here = dot(jnp.ones((8, TILE), F32), gather[...], trans_b=True)

    msg[0] = here[0:1]
    red1[j] = here[0:1]

    over_plane(msg.at[0], red1.at[j], 6, ar1)
    arrived(red1.at[pl.ds(0, COLS - 1)], ar1.at[0])
    part = sum_pairs(red1[...].reshape(COLS, TILE))
    msg[1] = part[0:1]
    red2[i] = part[0:1]

    for d in COLUMN:
        for other in (False, True):
            copy(msg.at[1], red2.at[i], sent.at[7], ar2.at[0], chip(d, other)).start()
    copy(msg.at[1], red2.at[i], sent.at[7], ar2.at[0], sib).start()
    arrived(red2.at[pl.ds(0, ROWS - 1)], ar2.at[0])

    sums = sum_pairs(red2[...].reshape(ROWS, TILE)) * (1.0 / TOTAL)

    g_km, g_km_low = pick(sums, 0, 1, 4, 0), pick(sums, 64, 1, 4, 0)
    f_ml = pick(sums, 16, 4, 0, 1)
    f_mk, f_mk_low = pick(sums, 16, 4, 1, 0), pick(sums, 80, 4, 1, 0)
    first, first_low = pltpu.roll(sums, TILE - 16, 1), pltpu.roll(sums, TILE - 80, 1)
    resid, resid_low = pltpu.roll(sums, TILE - 32, 1), pltpu.roll(sums, TILE - 96, 1)
    gf = (g_km[0] * f_ml[0] + g_km[1] * f_ml[1]) + (g_km[2] * f_ml[2] + g_km[3] * f_ml[3])
    alpha = first + (first - gf)
    a_ml, a_mk = pick(alpha, 0, 4, 0, 1), pick(alpha, 0, 4, 1, 0)
    p, e = -first, -first_low
    for m in range(K):
        q, r = two_prod(g_km[m], a_ml[m])
        p, t = two_sum(p, q)
        e = e + (r + t + g_km_low[m] * a_ml[m])
    p, e = two_sum(p, e)
    t_ml, t_ml_low = pick(p, 0, 4, 0, 1), pick(e, 0, 4, 0, 1)
    p, e = resid, resid_low
    for m in range(K):
        q, r = two_prod(-f_mk[m], a_ml[m])
        p, t = two_sum(p, q)
        e = e + (r + t - f_mk_low[m] * a_ml[m])
    for m in range(K):
        q, r = two_prod(a_mk[m], t_ml[m])
        p, t = two_sum(p, q)
        e = e + (r + t + a_mk[m] * t_ml_low[m])
    gram = p + e

    low = {}
    inv = []
    for k in range(K):
        d = entry(gram, k, k)
        for m in range(k):
            d = d - low[k, m] * low[k, m]
        inv.append(lax.rsqrt(d))
        low[k, k] = d * inv[k]
        for n in range(k + 1, K):
            v = entry(gram, n, k)
            for m in range(k):
                v = v - low[n, m] * low[k, m]
            low[n, k] = v * inv[k]

    done = []
    for l in range(K):
        r = res[l]
        for k in range(K):
            r = r - times(entry(alpha, k, l), x[k])
        for m in range(l):
            r = r - times(low[l, m], done[m])
        done.append(times(inv[l], r))
    for k in range(K):
        next_ref[:, k, :] = done[k]

    sub = lax.broadcasted_iota(jnp.int32, (8, TILE), 0)
    lane = lax.broadcasted_iota(jnp.int32, (8, TILE), 1)
    a, b = jnp.zeros((8, TILE), F32), jnp.zeros((8, TILE), F32)
    for k in range(K):
        for l in range(K):
            a = jnp.where((sub == k) & (lane == l), entry(alpha, k, l), a)
            if l >= k:
                b = jnp.where((sub == k) & (lane == l), low[l, k], b)
    alpha_ref[...] = a[0:K, 0:K]
    beta_ref[...] = b[0:K, 0:K]

    left(xcol.at[pl.ds(0, (CHIPS - 1) * CHUNK)], sent.at[0])
    left(xcol.at[pl.ds(0, CHIPS * CHUNK)], sent.at[1])
    left(fbuf.at[pl.ds(0, CHIPS - 1)], sent.at[2])
    left(fbuf.at[pl.ds(0, CHIPS)], sent.at[3])
    left(xrow.at[pl.ds(0, (COLS - 1) * CHUNK)], sent.at[4])
    left(dbuf.at[pl.ds(0, COLS - 1)], sent.at[5])
    left(red1.at[pl.ds(0, COLS - 1)], sent.at[6])
    left(red2.at[pl.ds(0, ROWS - 1)], sent.at[7])


def hand_over(*refs):
    n = len(refs) // 2
    sems = refs[-1]
    copies = [pltpu.make_async_copy(refs[k], refs[n + k], sems.at[k]) for k in range(n)]
    for c in copies:
        c.start()
    for c in copies:
        c.wait()


def step(tiles, tile_rows, tile_cols, tile_count, energy, basis_block, previous_block, coupling):
    vmem, hbm = (pl.BlockSpec(memory_space=m) for m in (pltpu.VMEM, pl.ANY))
    dma = pltpu.SemaphoreType.DMA
    def blocked(a):
        return a.reshape(K, BLOCKS, TILE).transpose(1, 0, 2)

    operands = (
        tile_rows, tile_cols, coupling, tiles, energy.reshape(BLOCKS, TILE),
        blocked(basis_block), blocked(previous_block),
    )
    out, alpha, beta = pl.pallas_call(
        body,
        out_shape=(
            pltpu.VMEM((BLOCKS, K, TILE), F32),
            pltpu.VMEM((K, K), F32),
            pltpu.VMEM((K, K), F32),
        ),
        in_specs=[pl.BlockSpec(memory_space=pltpu.SMEM)] + [hbm] * 7,
        out_specs=(vmem, vmem, vmem),
        scratch_shapes=[
            pltpu.SMEM((SLOTS,), jnp.int32),
            pltpu.SMEM((SLOTS,), jnp.int32),
            pltpu.SMEM((K, K), F32),
            pltpu.VMEM((ROWS * CHUNK, K, TILE), F32),
            pltpu.VMEM((COLS * CHUNK, K, TILE), F32),
            pltpu.VMEM((SLOTS, TILE, TILE), F32),
            pltpu.VMEM((SLOTS, 3 * TILE, TILE), jnp.bfloat16),
            pltpu.VMEM((SLOTS, 3 * TILE, TILE), jnp.bfloat16),
            pltpu.VMEM((BLOCKS, TILE), F32),
            pltpu.VMEM((BLOCKS, K, TILE), F32),
            pltpu.VMEM((K, SLOTS, TILE), F32),
            pltpu.VMEM((ROWS, K, SLOTS, TILE), F32),
            pltpu.VMEM((K, SLOTS, TILE), F32),
            pltpu.VMEM((COLS, K, SLOTS, TILE), F32),
            pltpu.VMEM((TILE, TILE), F32),
            pltpu.VMEM((COLS, 1, TILE), F32),
            pltpu.VMEM((ROWS, 1, TILE), F32),
            pltpu.VMEM((2, 1, TILE), F32),
            dma((8,)),
            dma((8,)),
            dma((CHIPS,)), dma((1,)), dma((1,)),
            dma((CHIPS,)), dma((1,)), dma((1,)),
            dma((1,)), dma((1,)),
        ],
        compiler_params=pltpu.CompilerParams(
            collective_id=0, has_side_effects=True, vmem_limit_bytes=32 << 20
        ),
        name="lanczos",
    )(tile_count, *(pltpu.with_memory_space_constraint(a, pltpu.HBM) for a in operands))
    results = (out, alpha, beta)
    out, alpha, beta = pl.pallas_call(
        hand_over,
        out_shape=tuple(jax.ShapeDtypeStruct(r.shape, F32) for r in results),
        in_specs=[hbm] * 3,
        out_specs=(hbm,) * 3,
        scratch_shapes=[dma((3,))],
        compiler_params=pltpu.CompilerParams(vmem_limit_bytes=1 << 20),
        name="hand_over",
    )(*results)
    return out.transpose(1, 0, 2).reshape(K, WIDTH), alpha, beta


def solution(mesh):
    both = ("row", "col")
    return jax.shard_map(
        step,
        mesh=mesh,
        in_specs=(
            P(both, None, None), P(both), P(both), P(both), P(both), P(None, both), P(None, both), P(),
        ),
        out_specs=(P(None, both), P(), P()),
        check_vma=False,
    )
```

```python
import jax
import jax.numpy as jnp
from jax import lax
from jax.experimental import pallas as pl
from jax.experimental.pallas import tpu as pltpu
from jax.sharding import PartitionSpec as P

MESH = pl.DeviceIdType.MESH
HIGH = lax.Precision.HIGHEST
F32 = jnp.float32
ROWS, COLS, CHIPS = 32, 16, 16
K, SLOTS, TILE, WIDTH = 4, 8, 128, 2048
BLOCKS = WIDTH // TILE
CHUNK = BLOCKS + 1
TOTAL = float(WIDTH * ROWS * COLS)
TREE = {
    0: (3, -3, 1, -1),
    3: (6, 4, 2), -3: (-6, -4, -2),
    6: (8, 7, 5), -6: (-7, -5),
}
WAVES = (3, -3, 1, -1), (6, -6, 2, -2, 4, -4), (5, -5, 7, -7, 8)
LIST_TREE = {0: (3, -3, 1, -1), 3: (6, 4, 2), -3: (-6, -4, -2), 6: (8, 7, 5), -6: (-7, -5)}
LIST_WAVES = ((3, -3, 1, -1), (6, -6, 2, -2, 4, -4), (5, -5, 7, -7, 8))
RING = {0: 0, 1: 1, 2: 2, 3: 1}
PLANE = sorted(
    ((dx, dy) for dx in range(4) for dy in range(4) if dx or dy), key=lambda p: -RING[p[0]] - RING[p[1]]
)
COLUMN = sorted(range(1, CHIPS), key=lambda d: -min(d, CHIPS - d))


def dot(a, b, trans_b=False):
    dims = (((1,), (1 if trans_b else 0,)), ((), ()))
    return lax.dot_general(a, b, dims, precision=HIGH, preferred_element_type=F32)


def thirds(a):
    parts = []
    for _ in range(3):
        p = a.astype(jnp.bfloat16).astype(F32)
        parts.append(p)
        a = a - p
    return parts


def split_tile(tile, out):
    for n, p in enumerate(thirds(tile)):
        out[n * TILE : (n + 1) * TILE, :] = p.astype(jnp.bfloat16)


def product(x, tile):
    left = jnp.concatenate(thirds(x) + [jnp.zeros_like(x)], axis=0).astype(jnp.bfloat16)
    y = lax.dot_general(
        jnp.concatenate([left] * 3, axis=1), tile, (((1,), (0,)), ((), ())), preferred_element_type=F32
    )
    return (y[8:12] + y[4:8]) + y[0:4]


def two_sum(a, b):
    s = a + b
    t = s - a
    return s, (a - (s - t)) + (b - t)


def split(a):
    c = a * 4097.0
    high = c - (c - a)
    return high, a - high


def two_prod(a, b):
    p = a * b
    ah, al = split(a)
    bh, bl = split(b)
    return p, ((ah * bh - p) + ah * bl + al * bh) + al * bl


def sum_pairs(rows):
    rows = [(jnp.broadcast_to(r, (8, TILE)), 0.0) for r in rows]
    while len(rows) > 1:
        pairs = []
        for (x, e), (y, f) in zip(rows[::2], rows[1::2]):
            x, r = two_sum(x, y)
            pairs.append((x, e + f + r))
        rows = pairs
    return rows[0]


def pick(row, base, stride_m, stride_k, stride_l):
    lane = lax.broadcasted_iota(jnp.int32, (8, TILE), 1)
    src = base + stride_k * (lane // 4 % 4) + stride_l * (lane % 4)
    return [jnp.take_along_axis(row, src + stride_m * m, axis=1, mode="promise_in_bounds") for m in range(K)]


def entry(row, k, l):
    src = jnp.full((8, TILE), 4 * k + l, jnp.int32)
    return jnp.take_along_axis(row, src, axis=1, mode="promise_in_bounds")


def times(v, plane):
    return (plane.reshape(2, 8, TILE) * v).reshape(BLOCKS, TILE)


def body(count, rows_hbm, cols_hbm, coupling_hbm, tiles_hbm, energy_hbm, basis_hbm, prev_hbm,
         next_ref, alpha_ref, beta_ref,
         rows, cols, coupling, xcol, xrow, tiles, parts, flipped, energy, prev, fbuf, dbuf, gather, red1, red2, msg,
         local, sent, xr, hr, pr, fr, gr, dr, ar1, ar2):
    i, j = lax.axis_index("row"), lax.axis_index("col")
    sib = (i + 1 - 2 * lax.rem(i, 2), j)

    def chip(d, other=False):
        core = lax.rem(i, 2)
        return (2 * lax.rem(i // 2 + d + CHIPS, CHIPS) + (1 - core if other else core), j)

    def plane(p):
        return (i, 4 * lax.rem(j // 4 + p[0], 4) + lax.rem(lax.rem(j, 4) + p[1], 4))

    def copy(src, dst, s, r, dev):
        return pltpu.make_async_remote_copy(
            src_ref=src, dst_ref=dst, send_sem=s, recv_sem=r, device_id=dev, device_id_type=MESH
        )

    def arrived(ref, sem):
        copy(ref, ref, sem, sem, sib).wait_recv()

    def left(ref, sem):
        copy(ref, ref, sem, sem, sib).wait_send()

    loads = [
        pltpu.make_async_copy(basis_hbm, xcol.at[pl.ds(i * CHUNK, BLOCKS)], local.at[0]),
        pltpu.make_async_copy(basis_hbm, xrow.at[pl.ds(j * CHUNK, BLOCKS)], local.at[1]),
        pltpu.make_async_copy(tiles_hbm, tiles, local.at[2]),
        pltpu.make_async_copy(energy_hbm, energy, local.at[3]),
        pltpu.make_async_copy(prev_hbm, prev, local.at[4]),
        pltpu.make_async_copy(rows_hbm, rows, local.at[5]),
        pltpu.make_async_copy(cols_hbm, cols, local.at[6]),
        pltpu.make_async_copy(coupling_hbm, coupling, local.at[7]),
    ]
    for c in loads:
        c.start()

    barrier = pltpu.get_barrier_semaphore()
    near = [chip(s * d) for d in (3, 2, 1) for s in (1, -1)] + [plane(p) for p in PLANE] + [sib]
    for dev in near:
        pl.semaphore_signal(barrier, inc=1, device_id=dev, device_id_type=MESH)

    for c in loads[5:]:
        c.wait()

    sub = lax.broadcasted_iota(jnp.int32, (K, TILE), 0)
    lane = lax.broadcasted_iota(jnp.int32, (K, TILE), 1)
    places = jnp.zeros((K, TILE), F32)
    for t in range(SLOTS):
        live = jnp.full((K, TILE), t, jnp.int32) < jnp.full((K, TILE), count[0], jnp.int32)
        c = jnp.where(live, jnp.full((K, TILE), cols[t], jnp.int32), -1).astype(F32)
        r = jnp.where(live, jnp.full((K, TILE), rows[t], jnp.int32), -1).astype(F32)
        places = jnp.where((sub == i // 16) & (lane == lax.rem(i, 16) * SLOTS + t), c, places)
        places = jnp.where((sub == 2) & (lane == j * SLOTS + t), r, places)
    xcol[i * CHUNK + BLOCKS] = places
    xrow[j * CHUNK + BLOCKS] = places
    loads[0].wait()
    loads[1].wait()
    pl.semaphore_wait(barrier, len(near))

    def place(buf, t):
        slot = lax.rem(i - 2 * t + ROWS, ROWS)
        return buf.at[pl.ds(slot * CHUNK, CHUNK)] if buf is xcol else buf.at[slot]

    def onward(buf, n, rsem, hsem, t):
        at = place(buf, t)
        for u in (TREE if buf is xcol else LIST_TREE).get(t, ()):
            copy(at, at, sent.at[n], rsem.at[u + CHIPS // 2 - 1], chip(u - t)).start()
        copy(at, at, sent.at[n + 1], hsem.at[0], sib).start()

    def arrive(buf, n, rsem, hsem, hops):
        for t in hops:
            arrived(place(buf, t), rsem.at[t + CHIPS // 2 - 1])
            onward(buf, n, rsem, hsem, t)

    def over_plane(src, dst, n, rsem):
        for p in PLANE:
            copy(src, dst, sent.at[n], rsem.at[0], plane(p)).start()

    own = xrow.at[pl.ds(j * CHUNK, CHUNK)]
    onward(xcol, 0, xr, hr, 0)
    over_plane(own, own, 4, pr)

    for c in loads[2:5]:
        c.wait()
    for t in range(SLOTS):
        split_tile(tiles[t], parts.at[t])

    for t in range(SLOTS):
        split_tile(tiles[t].T, flipped.at[t])
    arrive(xcol, 0, xr, hr, WAVES[0])
    arrived(xrow.at[pl.ds(0, (COLS - 1) * CHUNK)], pr.at[0])

    for t in range(SLOTS):
        r = rows[t]
        v = xrow[r + lax.shift_right_logical(r, 4)]
        y = product(v, parts[t])
        for k in range(K):
            fbuf[i, k, t : t + 1, :] = y[k : k + 1, :]
    onward(fbuf, 2, fr, gr, 0)

    arrive(xcol, 0, xr, hr, WAVES[1])
    arrive(fbuf, 2, fr, gr, LIST_WAVES[0])
    arrive(xcol, 0, xr, hr, WAVES[2])
    arrived(xcol.at[pl.ds(0, ROWS // 2 * CHUNK)], hr.at[0])

    for t in range(SLOTS):
        r = cols[t]
        v = xcol[r + lax.shift_right_logical(r, 4)]
        y = product(v, flipped[t])
        for k in range(K):
            dbuf[j, k, t : t + 1, :] = y[k : k + 1, :]
    over_plane(dbuf.at[j], dbuf.at[j], 5, dr)
    arrive(fbuf, 2, fr, gr, LIST_WAVES[1])

    at_cols = jnp.zeros((K, TILE), F32)
    for d in range(ROWS):
        at_cols = at_cols + xcol[d * CHUNK + BLOCKS]
    at_rows = jnp.zeros((K, TILE), F32)
    for d in range(COLS):
        at_rows = at_rows + xrow[d * CHUNK + BLOCKS]
    block = lax.broadcasted_iota(jnp.int32, (BLOCKS, TILE), 0)

    def hot(line, first):
        return jnp.where(line.astype(jnp.int32) == block + first * BLOCKS, 1.0, 0.0).astype(F32)

    hot_low = hot(at_cols[0:1, :], i)
    hot_high = hot(at_cols[1:2, :], i)
    hot_row = hot(at_rows[2:3, :], j)

    x = [xcol[pl.ds(i * CHUNK, BLOCKS), k, :] for k in range(K)]
    old = [prev[:, k, :] for k in range(K)]
    res = []
    for k in range(K):
        r = energy[...] * x[k]
        for m in range(K):
            r = r - coupling[k, m] * old[m]
        res.append(r)

    gather[...] = jnp.zeros((TILE, TILE), F32)

    def inner(row, a, b):
        gather[row : row + 1, :] = jnp.sum(a * b, axis=0, keepdims=True)

    for k in range(K):
        for l in range(K):
            inner(4 * k + l, x[k], x[l])

    arrive(fbuf, 2, fr, gr, LIST_WAVES[2])
    arrived(fbuf.at[pl.ds(0, ROWS // 2)], gr.at[0])
    for k in range(K):
        low = fbuf[0:16, k].reshape(TILE, TILE)
        high = fbuf[16:32, k].reshape(TILE, TILE)
        res[k] = res[k] + (dot(hot_low, low) + dot(hot_high, high))
    arrived(dbuf.at[pl.ds(0, COLS - 1)], dr.at[0])
    for k in range(K):
        res[k] = res[k] + dot(hot_row, dbuf[:, k].reshape(TILE, TILE))

    for k in range(K):
        for l in range(K):
            inner(16 + 4 * k + l, x[k], res[l])
            if k <= l:
                both = jnp.sum(res[k] * res[l], axis=0, keepdims=True)
                gather[32 + 4 * k + l : 33 + 4 * k + l, :] = both
                gather[32 + 4 * l + k : 33 + 4 * l + k, :] = both
    here = dot(jnp.ones((8, TILE), F32), gather[...], trans_b=True)

    msg[0] = here[0:1]
    red1[j] = here[0:1]

    over_plane(msg.at[0], red1.at[j], 6, ar1)
    arrived(red1.at[pl.ds(0, COLS - 1)], ar1.at[0])
    part, lost = sum_pairs([red1[n] for n in range(COLS)])
    lane = lax.broadcasted_iota(jnp.int32, (8, TILE), 1)
    part = part + jnp.where(lane >= 64, pltpu.roll(lost, 64, 1), 0.0)
    msg[1] = part[0:1]
    red2[i] = part[0:1]

    for d in COLUMN:
        for other in (False, True):
            copy(msg.at[1], red2.at[i], sent.at[7], ar2.at[0], chip(d, other)).start()
    copy(msg.at[1], red2.at[i], sent.at[7], ar2.at[0], sib).start()
    arrived(red2.at[pl.ds(0, ROWS - 1)], ar2.at[0])

    sums, lost = sum_pairs([red2[n] for n in range(ROWS)])
    sums, lost = sums * (1.0 / TOTAL), lost * (1.0 / TOTAL)

    def pick_low(base, *strides):
        return [a + b for a, b in zip(pick(sums, 64 + base, *strides), pick(lost, base, *strides))]

    def moved(base):
        low = pltpu.roll(sums, TILE - 64 - base, 1) + pltpu.roll(lost, TILE - base, 1)
        return pltpu.roll(sums, TILE - base, 1), low

    g_km, g_km_low = pick(sums, 0, 1, 4, 0), pick_low(0, 1, 4, 0)
    f_ml = pick(sums, 16, 4, 0, 1)
    f_mk, f_mk_low = pick(sums, 16, 4, 1, 0), pick_low(16, 4, 1, 0)
    (first, first_low), (resid, resid_low) = moved(16), moved(32)
    gf = (g_km[0] * f_ml[0] + g_km[1] * f_ml[1]) + (g_km[2] * f_ml[2] + g_km[3] * f_ml[3])
    alpha = first + (first - gf)
    a_ml, a_mk = pick(alpha, 0, 4, 0, 1), pick(alpha, 0, 4, 1, 0)
    p, e = -first, -first_low
    for m in range(K):
        q, r = two_prod(g_km[m], a_ml[m])
        p, t = two_sum(p, q)
        e = e + (r + t + g_km_low[m] * a_ml[m])
    p, e = two_sum(p, e)
    t_ml, t_ml_low = pick(p, 0, 4, 0, 1), pick(e, 0, 4, 0, 1)
    p, e = resid, resid_low
    for m in range(K):
        q, r = two_prod(-f_mk[m], a_ml[m])
        p, t = two_sum(p, q)
        e = e + (r + t - f_mk_low[m] * a_ml[m])
    for m in range(K):
        q, r = two_prod(a_mk[m], t_ml[m])
        p, t = two_sum(p, q)
        e = e + (r + t + a_mk[m] * t_ml_low[m])
    gram = p + e

    low = {}
    inv = []
    for k in range(K):
        d = entry(gram, k, k)
        for m in range(k):
            d = d - low[k, m] * low[k, m]
        inv.append(lax.rsqrt(d))
        low[k, k] = d * inv[k]
        for n in range(k + 1, K):
            v = entry(gram, n, k)
            for m in range(k):
                v = v - low[n, m] * low[k, m]
            low[n, k] = v * inv[k]

    done = []
    for l in range(K):
        r = res[l]
        for k in range(K):
            r = r - times(entry(alpha, k, l), x[k])
        for m in range(l):
            r = r - times(low[l, m], done[m])
        done.append(times(inv[l], r))
    for k in range(K):
        next_ref[:, k, :] = done[k]

    sub = lax.broadcasted_iota(jnp.int32, (8, TILE), 0)
    lane = lax.broadcasted_iota(jnp.int32, (8, TILE), 1)
    a, b = jnp.zeros((8, TILE), F32), jnp.zeros((8, TILE), F32)
    for k in range(K):
        for l in range(K):
            a = jnp.where((sub == k) & (lane == l), entry(alpha, k, l), a)
            if l >= k:
                b = jnp.where((sub == k) & (lane == l), low[l, k], b)
    alpha_ref[...] = a[0:K, 0:K]
    beta_ref[...] = b[0:K, 0:K]

    left(xcol.at[pl.ds(0, (CHIPS - 1) * CHUNK)], sent.at[0])
    left(xcol.at[pl.ds(0, CHIPS * CHUNK)], sent.at[1])
    left(fbuf.at[pl.ds(0, CHIPS - 1)], sent.at[2])
    left(fbuf.at[pl.ds(0, CHIPS)], sent.at[3])
    left(xrow.at[pl.ds(0, (COLS - 1) * CHUNK)], sent.at[4])
    left(dbuf.at[pl.ds(0, COLS - 1)], sent.at[5])
    left(red1.at[pl.ds(0, COLS - 1)], sent.at[6])
    left(red2.at[pl.ds(0, ROWS - 1)], sent.at[7])


def hand_over(*refs):
    n = len(refs) // 2
    sems = refs[-1]
    copies = [pltpu.make_async_copy(refs[k], refs[n + k], sems.at[k]) for k in range(n)]
    for c in copies:
        c.start()
    for c in copies:
        c.wait()


def step(tiles, tile_rows, tile_cols, tile_count, energy, basis_block, previous_block, coupling):
    vmem, hbm = (pl.BlockSpec(memory_space=m) for m in (pltpu.VMEM, pl.ANY))
    dma = pltpu.SemaphoreType.DMA
    def blocked(a):
        return a.reshape(K, BLOCKS, TILE).transpose(1, 0, 2)

    operands = (
        tile_rows, tile_cols, coupling, tiles, energy.reshape(BLOCKS, TILE),
        blocked(basis_block), blocked(previous_block),
    )
    out, alpha, beta = pl.pallas_call(
        body,
        out_shape=(
            pltpu.VMEM((BLOCKS, K, TILE), F32),
            pltpu.VMEM((K, K), F32),
            pltpu.VMEM((K, K), F32),
        ),
        in_specs=[pl.BlockSpec(memory_space=pltpu.SMEM)] + [hbm] * 7,
        out_specs=(vmem, vmem, vmem),
        scratch_shapes=[
            pltpu.SMEM((SLOTS,), jnp.int32),
            pltpu.SMEM((SLOTS,), jnp.int32),
            pltpu.SMEM((K, K), F32),
            pltpu.VMEM((ROWS * CHUNK, K, TILE), F32),
            pltpu.VMEM((COLS * CHUNK, K, TILE), F32),
            pltpu.VMEM((SLOTS, TILE, TILE), F32),
            pltpu.VMEM((SLOTS, 3 * TILE, TILE), jnp.bfloat16),
            pltpu.VMEM((SLOTS, 3 * TILE, TILE), jnp.bfloat16),
            pltpu.VMEM((BLOCKS, TILE), F32),
            pltpu.VMEM((BLOCKS, K, TILE), F32),
            pltpu.VMEM((ROWS, K, SLOTS, TILE), F32),
            pltpu.VMEM((COLS, K, SLOTS, TILE), F32),
            pltpu.VMEM((TILE, TILE), F32),
            pltpu.VMEM((COLS, 1, TILE), F32),
            pltpu.VMEM((ROWS, 1, TILE), F32),
            pltpu.VMEM((2, 1, TILE), F32),
            dma((8,)),
            dma((8,)),
            dma((CHIPS,)), dma((1,)), dma((1,)),
            dma((CHIPS,)), dma((1,)), dma((1,)),
            dma((1,)), dma((1,)),
        ],
        compiler_params=pltpu.CompilerParams(
            collective_id=0, has_side_effects=True, vmem_limit_bytes=32 << 20
        ),
        name="lanczos",
    )(tile_count, *(pltpu.with_memory_space_constraint(a, pltpu.HBM) for a in operands))
    results = (out, alpha, beta)
    out, alpha, beta = pl.pallas_call(
        hand_over,
        out_shape=tuple(jax.ShapeDtypeStruct(r.shape, F32) for r in results),
        in_specs=[hbm] * 3,
        out_specs=(hbm,) * 3,
        scratch_shapes=[dma((3,))],
        compiler_params=pltpu.CompilerParams(vmem_limit_bytes=1 << 20),
        name="hand_over",
    )(*results)
    return out.transpose(1, 0, 2).reshape(K, WIDTH), alpha, beta


def solution(mesh):
    both = ("row", "col")
    return jax.shard_map(
        step,
        mesh=mesh,
        in_specs=(
            P(both, None, None), P(both), P(both), P(both), P(both), P(None, both), P(None, both), P(),
        ),
        out_specs=(P(None, both), P(), P()),
        check_vma=False,
    )
```
